256 devices in a mesh: samp: 2 (over y_lo), row: 8 (over y_hi, x), col: 16 (over z, core).
Axes of the slice: x: 4, y: 4 (y_hi: 2, y_lo: 2; y = y_hi * 2 + y_lo), z: 8, core: 2. Of those that a mesh axis runs over, the one named last changes fastest.
Arguments:
- tokens: bfloat16 [8, 1024, 768], P('samp', 'col'), may hold values from -110 to 110
- restype: int32 [1024], P('col'), may hold values from 0 to 31
- type_table: bfloat16 [32, 768], replicated, may hold values from -8 to 8
- key_mask: int32 [1024], P('col'), may hold values 0 or 1
- pair: bfloat16 [1024, 1024, 128], P('row', 'col'), may hold values from -160 to 160
- w_bias: bfloat16 [128, 16], replicated, may hold values from -0.5 to 0.5
- w_query: bfloat16 [768, 768], replicated, may hold values from -2 to 2
- w_key: bfloat16 [768, 768], replicated, may hold values from -2 to 2
- w_value: bfloat16 [768, 768], replicated, may hold values from -0.21875 to 0.21875
- w_gate: bfloat16 [768, 768], replicated, may hold values from -0.21875 to 0.21875
- cotangent: bfloat16 [8, 1024, 768], P('samp', 'col'), may hold values from -6 to 6
Outputs:
- token_grad: bfloat16 [8, 1024, 768], P('samp', 'col')
- pair_grad: bfloat16 [1024, 1024, 128], P('row', 'col')
- bias_weight_grad: float32 [128, 16], replicated
The draws below stay inside these ranges and needn't reach their ends.
All inputs are finite; a program needn't handle non-finite values. No bound on the sum of `key_mask` on one device may be relied on, other than what follows from the above.
Results may differ from the reference program's by a relative error of at most 0.034.
The reference program's roundings to bfloat16 on the way count: a program that leaves them out, or rounds other values in their place, can miss the bound.
Values may be sent and summed in bfloat16 or wider, within the bound.
A program may use at most 128 MiB of HBM per device.

```python
import math
import jax
import jax.numpy as jnp
from jax import lax

D = 768
H = 16
CH = 48
C = 128
NTYPE = 32
TOKENS = 1024
SAMPLES = 8
N_ROW = 8


def shared_base(key):
    return jnp.clip(jax.random.normal(jax.random.fold_in(key, 21), (D, D), jnp.float32), -5.0, 5.0)


def draw_tokens(key, part):
    key = jax.random.fold_in(key, 11)
    first, second, third = jax.random.split(key, 3)
    channel_scale = jnp.exp(jax.random.uniform(second, (D,), jnp.float32) * math.log(10.0))
    token_scale = jnp.exp(jax.random.uniform(third, (SAMPLES, TOKENS, 1), jnp.float32) * math.log(2.0))
    base = jnp.clip(jax.random.normal(first, (SAMPLES, TOKENS, D), jnp.float32), -5.0, 5.0)
    return (base * channel_scale * token_scale).astype(jnp.bfloat16)


def draw_pair(key, part):
    key = jax.random.fold_in(key, 12)
    first, second, third = jax.random.split(key, 3)
    channel_scale = jnp.exp(jax.random.uniform(second, (C,), jnp.float32) * math.log(10.0))
    row_scale = jnp.exp(jax.random.uniform(third, (TOKENS, 1, 1), jnp.float32) * math.log(3.0))
    base = jnp.clip(jax.random.normal(first, (TOKENS, TOKENS, C), jnp.float32), -5.0, 5.0)
    return (base * channel_scale * row_scale).astype(jnp.bfloat16)


def draw_w_query(key, part):
    base = shared_base(key)
    return (base / math.sqrt(D)).astype(jnp.bfloat16)


def draw_w_key(key, part):
    key = jax.random.fold_in(key, 32)
    fresh = jnp.clip(jax.random.normal(key, (D, D), jnp.float32), -5.0, 5.0)
    return (fresh / math.sqrt(D)).astype(jnp.bfloat16)


def touch_ends(drawn, key, smallest, top_value):
    longest = drawn.shape.index(max(drawn.shape))
    spots = []
    for shift in (0, 1):
        where = [jax.random.randint(jax.random.fold_in(key, axis), (), 0, length) for axis, length in enumerate(drawn.shape)]
        where[longest] = (where[longest] + shift) % drawn.shape[longest]
        spots.append(tuple(where))
    return drawn.at[spots[0]].set(smallest).at[spots[1]].set(top_value)


def steps_of(key, shape, cuts, smallest, high):
    def one(dim, parts):
        draws = jax.random.uniform(jax.random.fold_in(jax.random.fold_in(key, 6), dim), (parts,), jnp.float32, smallest / len(cuts), high / len(cuts))
        return jnp.repeat(jnp.exp(draws), shape[dim] // parts).reshape((-1,) + (1,) * (len(shape) - dim - 1))

    level = one(*cuts[0])
    for cut in cuts[1:]:
        level = level * one(*cut)
    return level


def noise(key, dims, spread, reach, shards=(), kind=jnp.bfloat16):
    gain = steps_of(key, dims, shards, -0.22, 0.18) if shards else 1.0
    entries = jax.random.normal(key, dims, jnp.float32) * spread * gain
    return jnp.minimum(jnp.maximum(entries, -reach), reach).astype(kind)


def setup_inputs(seed: int = 0) -> dict:
    key_of = jax.random.split(jax.random.key(seed), 12)
    return {
        "tokens": draw_tokens(jax.random.fold_in(key_of[11], 71), 0),
        "restype": touch_ends(jax.random.randint(key_of[1], (TOKENS,), 0, NTYPE), jax.random.fold_in(key_of[1], 1), 0, NTYPE - 1).astype(jnp.int32),
        "type_table": noise(key_of[2], (NTYPE, D), 2.0, 8.0),
        "key_mask": touch_ends((jax.random.randint(key_of[3], (TOKENS,), 0, 8) < 7).astype(jnp.int32), jax.random.fold_in(key_of[3], 1), 0, 1),
        "pair": draw_pair(jax.random.fold_in(key_of[11], 71), 0),
        "w_bias": noise(key_of[5], (C, H), C ** -0.5, 0.5),
        "w_query": draw_w_query(jax.random.fold_in(key_of[11], 71), 0),
        "w_key": draw_w_key(jax.random.fold_in(key_of[11], 71), 0),
        "w_value": noise(key_of[8], (D, D), D ** -0.5, 0.21875),
        "w_gate": noise(key_of[9], (D, D), D ** -0.5, 0.21875),
        "cotangent": noise(key_of[10], (SAMPLES, TOKENS, D), 1.0, 6.0, ((0, 2), (1, 16))),
    }


def token_norm(tokens, restype, type_table):
    onehot = (restype[:, None] == jnp.arange(NTYPE, dtype=jnp.int32)[None, :]).astype(jnp.bfloat16)
    embedded = tokens.astype(jnp.float32) + jnp.dot(onehot, type_table, preferred_element_type=jnp.float32)
    centred = embedded - lax.optimization_barrier(jnp.mean(embedded, axis=-1, keepdims=True))
    inv_std = lax.rsqrt(lax.optimization_barrier(jnp.mean(centred * centred, axis=-1, keepdims=True)) + 1e-05)
    return (centred * inv_std, inv_std)

def pair_norm(block):
    values = block.astype(jnp.float32)
    centred = values - lax.optimization_barrier(jnp.mean(values, axis=-1, keepdims=True))
    inv_std = lax.rsqrt(lax.optimization_barrier(jnp.mean(centred * centred, axis=-1, keepdims=True)) + 1e-05)
    return (centred * inv_std, inv_std)

def norm_back(grad_in, normed, inv_std):
    return inv_std * (grad_in - lax.optimization_barrier(jnp.mean(grad_in, axis=-1, keepdims=True)) - normed * lax.optimization_barrier(jnp.mean(grad_in * normed, axis=-1, keepdims=True)))

def reference(tokens, restype, type_table, key_mask, pair, w_bias, w_query, w_key, w_value, w_gate, cotangent):
    normed, inv_std = token_norm(tokens, restype, type_table)
    act = normed.astype(jnp.bfloat16)
    bias_weight = w_bias.astype(jnp.float32)
    block_rows = TOKENS // N_ROW
    blocks = pair.reshape(N_ROW, block_rows, TOKENS, C)

    def block_bias(block):
        pair_normed, pair_inv = pair_norm(block)
        return jnp.einsum('ijc,ch->hij', pair_normed, bias_weight, precision=lax.Precision.HIGHEST)
    bias = lax.map(block_bias, blocks)
    bias = jnp.transpose(bias, (1, 0, 2, 3)).reshape(H, TOKENS, TOKENS)
    keep = key_mask == 1
    w_query_f = w_query.astype(jnp.float32)
    w_key_f = w_key.astype(jnp.float32)
    w_value_f = w_value.astype(jnp.float32)

    def one_sample(grad_bias, inputs):
        act_s, grad_s = inputs
        queries = jnp.dot(act_s, w_query, preferred_element_type=jnp.float32).astype(jnp.bfloat16)
        key_proj = jnp.dot(act_s, w_key, preferred_element_type=jnp.float32).astype(jnp.bfloat16)
        value_proj = jnp.dot(act_s, w_value, preferred_element_type=jnp.float32).astype(jnp.bfloat16)
        gate_lin = jnp.dot(act_s, w_gate, preferred_element_type=jnp.float32).astype(jnp.bfloat16)
        query_heads = queries.astype(jnp.float32).reshape(TOKENS, H, CH)
        key_heads = key_proj.astype(jnp.float32).reshape(TOKENS, H, CH)
        value_heads = value_proj.astype(jnp.float32).reshape(TOKENS, H, CH)
        scores = jnp.einsum('ihc,jhc->hij', query_heads, key_heads) / math.sqrt(CH) + bias
        scores = jnp.where(keep[None, None, :], scores, -1000000000.0)
        top = lax.optimization_barrier(jnp.max(scores, axis=-1, keepdims=True))
        expo = jnp.exp(scores - top)
        totals = lax.optimization_barrier(jnp.sum(expo, axis=-1))
        attended = jnp.einsum('hij,jhc->ihc', expo.astype(jnp.bfloat16).astype(jnp.float32), value_heads)
        attended = attended / jnp.transpose(totals)[:, :, None]
        flat_out = attended.reshape(TOKENS, D)
        sig_gate = jax.nn.sigmoid(gate_lin.astype(jnp.float32))
        grad_f = grad_s.astype(jnp.float32)
        grad_out = (grad_f * sig_gate).astype(jnp.bfloat16)
        grad_gate = (grad_f * flat_out * sig_gate * (1.0 - sig_gate)).astype(jnp.bfloat16)
        grad_heads = grad_out.astype(jnp.float32).reshape(TOKENS, H, CH)
        delta = jnp.transpose(lax.optimization_barrier(jnp.sum(grad_heads * attended, axis=-1)))
        probs = expo / totals[:, :, None]
        grad_pre = jnp.einsum('ihc,jhc->hij', grad_heads, value_heads)
        grad_scores = probs * (grad_pre - delta[:, :, None])
        rounded = grad_scores.astype(jnp.bfloat16).astype(jnp.float32)
        grad_query = (jnp.einsum('hij,jhc->ihc', rounded, key_heads) / math.sqrt(CH)).reshape(TOKENS, D)
        grad_key = (jnp.einsum('hij,ihc->jhc', rounded, query_heads) / math.sqrt(CH)).reshape(TOKENS, D)
        grad_value = jnp.einsum('hij,ihc->jhc', probs.astype(jnp.bfloat16).astype(jnp.float32), grad_heads).reshape(TOKENS, D)
        grad_act = jnp.dot(grad_query, w_query_f.T, precision=lax.Precision.HIGHEST)
        grad_act = grad_act + jnp.dot(grad_key, w_key_f.T, precision=lax.Precision.HIGHEST)
        grad_act = grad_act + jnp.dot(grad_value, w_value_f.T, precision=lax.Precision.HIGHEST)
        grad_act = grad_act + jnp.dot(grad_gate, w_gate.T, preferred_element_type=jnp.float32)
        return (grad_bias + grad_scores, grad_act)
    grad_bias, grad_act = lax.scan(one_sample, jnp.zeros((H, TOKENS, TOKENS), jnp.float32), (act, cotangent))
    token_grad = norm_back(grad_act, normed, inv_std).astype(jnp.bfloat16)
    bias_blocks = jnp.transpose(grad_bias.reshape(H, N_ROW, block_rows, TOKENS), (1, 0, 2, 3))

    def block_grads(inputs):
        block, grad_block = inputs
        pair_normed, pair_inv = pair_norm(block)
        grad_normed = jnp.einsum('hij,ch->ijc', grad_block, bias_weight, precision=lax.Precision.HIGHEST)
        grad_pair = norm_back(grad_normed, pair_normed, pair_inv)
        weight_part = jnp.einsum('ijc,hij->ch', pair_normed, grad_block, precision=lax.Precision.HIGHEST)
        return ((grad_pair * (TOKENS / SAMPLES)).astype(jnp.bfloat16), weight_part)
    pair_blocks, weight_parts = lax.map(block_grads, (blocks, bias_blocks))
    pair_grad = pair_blocks.reshape(TOKENS, TOKENS, C)
    bias_weight_grad = lax.optimization_barrier(jnp.sum(weight_parts, axis=0)) / SAMPLES
    return (token_grad, pair_grad, bias_weight_grad)
```

```python
import functools
import math

import jax
import jax.numpy as jnp
from jax import lax
from jax.experimental import pallas as pl
from jax.experimental.pallas import tpu as pltpu
from jax.sharding import PartitionSpec as P

D = 768
H = 16
CH = 48
C = 128
NTYPE = 32
GROUP = 4
NG = H // GROUP
GW = GROUP * CH
EPS = 1e-05
NEG = -1000000000.0
BF = jnp.bfloat16
F32 = jnp.float32
MESH = pl.DeviceIdType.MESH


def dot_nn(a, b):
    return jnp.dot(a, b, preferred_element_type=F32)


def dot_nt(a, b):
    return lax.dot_general(a, b, (((1,), (1,)), ((), ())), preferred_element_type=F32)


def dot_tn(a, b):
    return lax.dot_general(a, b, (((0,), (0,)), ((), ())), preferred_element_type=F32)


def split(x):
    high = x.astype(BF)
    return high, (x - high.astype(F32)).astype(BF)


def norm(x):
    centred = x - jnp.mean(x, axis=-1, keepdims=True)
    inv = lax.rsqrt(jnp.mean(centred * centred, axis=-1, keepdims=True) + EPS)
    return centred * inv, inv


def norm_back(grad, normed, inv):
    return inv * (
        grad
        - jnp.mean(grad, axis=-1, keepdims=True)
        - normed * jnp.mean(grad * normed, axis=-1, keepdims=True)
    )


def kernel(
    sizes,
    tok_ref,
    rest_ref,
    table_ref,
    mask_ref,
    wbt_ref,
    cot_ref,
    wq_hbm,
    wk_hbm,
    wv_hbm,
    wg_hbm,
    pair_hbm,
    tg_ref,
    bw_ref,
    pg_hbm,
    wq_ref,
    wk_ref,
    wv_ref,
    wg_ref,
    pair_ref,
    raw_ref,
    nrm_ref,
    inv_ref,
    bias_ref,
    emb_ref,
    act_ref,
    k_ref,
    v_ref,
    sig_ref,
    qgs_ref,
    qg_ref,
    bdm_ref,
    keep_ref,
    e_ref,
    dp_ref,
    ot_ref,
    st_ref,
    str_ref,
    res_ref,
    resr_ref,
    gb_ref,
    gbr_ref,
    dkv_ref,
    ekv_ref,
    od_ref,
    ods_ref,
    dqs_ref,
    dqr_ref,
    os_ref,
    or_ref,
    pm_ref,
    pmr_ref,
    wg_acc_ref,
    hr_ref,
    hs_ref,
    hr2_ref,
    w_sem,
    pair_sem,
    out_sem,
    t_sem,
    ag_send,
    ag_recv,
    sib_send,
    sib_recv,
    b_send,
    b_recv,
    b2_send,
    b2_recv,
    e_send,
    e_recv,
    x_send,
    x_recv,
    d_send,
    d_recv,
    o_send,
    o_recv,
    f_sem,
    pm_sem,
    g_send,
    g_recv,
    h_send,
    h_recv,
    h2_send,
    h2_recv,
):
    n_row, n_col, total_tokens, samples = sizes
    samp = lax.axis_index("samp")
    row = lax.axis_index("row")
    col = lax.axis_index("col")
    core = lax.rem(col, 2)
    z = col // 2
    n_z = n_col // 2
    scale = 1.0 / math.sqrt(CH)
    rest_row = row // 2
    own_tok = pl.multiple_of(lax.rem(row, 2) * 32, 32)

    def at_col(c):
        return (samp, row, c)

    def at_row(r):
        return (samp, r, col)

    sibling = at_col(z * 2 + 1 - core)
    swapped = (samp, z, row * 2 + core)
    is_diag = row == z
    other_samp = (1 - samp, row, col)

    def remote(src, dst, send, recv, device):
        return pltpu.make_async_remote_copy(
            src_ref=src,
            dst_ref=dst,
            send_sem=send,
            recv_sem=recv,
            device_id=device,
            device_id_type=MESH,
        )

    weights = [
        pltpu.make_async_copy(src, dst, w_sem.at[n])
        for n, (src, dst) in enumerate(
            ((wq_hbm, wq_ref), (wg_hbm, wg_ref), (wk_hbm, wk_ref), (wv_hbm, wv_ref))
        )
    ]
    for copy in weights:
        copy.start()
    pair_copy = pltpu.make_async_copy(pair_hbm, pair_ref, pair_sem)
    pair_copy.start()

    barrier = pltpu.get_barrier_semaphore()

    def greet(device):
        pl.semaphore_signal(barrier, inc=1, device_id=device, device_id_type=MESH)

    def greet_col(d, carry):
        greet(at_col(lax.rem(col + d, n_col)))
        return carry

    def greet_row(d, carry):
        greet(at_row(lax.rem(row + d, n_row)))
        return carry

    lax.fori_loop(1, n_col, greet_col, 0)
    lax.fori_loop(1, n_row, greet_row, 0)
    greet(other_samp)

    @pl.when(jnp.logical_not(is_diag))
    def _():
        greet(swapped)

    onehot = (rest_ref[...] == lax.broadcasted_iota(jnp.int32, (64, NTYPE), 1)).astype(F32)
    emb_ref[...] = dot_nn(onehot.astype(BF), table_ref[...])
    own_rows = pl.ds(own_tok, 32)
    own_normed, own_inv = norm(tok_ref[rest_row, own_rows, :].astype(F32) + emb_ref[own_rows, :])
    own_act = own_normed.astype(BF)
    weights[0].wait()
    qgs_ref[0] = dot_nn(own_act, wq_ref[...]).astype(BF)
    weights[1].wait()
    gate = dot_nn(own_act, wg_ref[...]).astype(BF).astype(F32)
    sig = jax.nn.sigmoid(gate)
    sig_ref[...] = sig
    own_cot = cot_ref[rest_row, own_rows, :].astype(F32)
    qgs_ref[1] = (own_cot * sig).astype(BF)

    @pl.when(is_diag)
    def _():
        pl.semaphore_wait(barrier, n_col + n_row - 1)

    @pl.when(jnp.logical_not(is_diag))
    def _():
        pl.semaphore_wait(barrier, n_col + n_row)

    def region(zz, kk):
        start = pl.multiple_of(kk * 64 + lax.rem(zz, 2) * 32, 32)
        return qg_ref.at[zz // 2, :, pl.ds(start, 32), :]

    to_swapped = remote(qgs_ref, region(row, core), t_sem.at[0], t_sem.at[1], swapped)
    from_swapped = remote(qgs_ref, region(z, core), t_sem.at[0], t_sem.at[1], swapped)
    keep_own = pltpu.make_async_copy(qgs_ref, region(z, core), t_sem.at[2])

    @pl.when(jnp.logical_not(is_diag))
    def _():
        to_swapped.start()

    @pl.when(is_diag)
    def _():
        keep_own.start()

    weights[2].wait()
    weights[3].wait()

    def project(s, carry):
        normed, _ = norm(tok_ref[s].astype(F32) + emb_ref[...])
        act = normed.astype(BF)
        k_ref[s] = dot_nn(act, wk_ref[...]).astype(BF)
        v_ref[s] = dot_nn(act, wv_ref[...]).astype(BF)
        return carry

    lax.fori_loop(0, 4, project, 0)
    lane = lax.broadcasted_iota(jnp.int32, (64, GW), 1)
    for h in range(GROUP):
        inside = jnp.logical_and(lane >= h * CH, lane < (h + 1) * CH)
        bdm_ref[h * 64 : (h + 1) * 64, :] = jnp.where(inside, 1.0, 0.0).astype(BF)
    keep_ref[...] = jnp.where(mask_ref[...] == 1, 1.0, 0.0) * jnp.ones((64, 128), F32)

    @pl.when(jnp.logical_not(is_diag))
    def _():
        to_swapped.wait_send()
        from_swapped.wait_recv()

    @pl.when(is_diag)
    def _():
        keep_own.wait()

    def ag_copy(d):
        zz = lax.rem(z + d, n_z)
        return remote(
            region(z, core), region(z, core), ag_send.at[d], ag_recv.at[z], at_col(zz * 2 + core)
        )

    def ag_wait(zz):
        return remote(
            region(zz, core), region(zz, core), ag_send.at[0], ag_recv.at[zz], sibling
        )

    def sib_copy(zz):
        return remote(
            region(zz, core), region(zz, core), sib_send.at[zz], sib_recv.at[zz], sibling
        )

    def sib_wait(zz):
        return remote(
            region(zz, 1 - core), region(zz, 1 - core), sib_send.at[zz], sib_recv.at[zz], sibling
        )

    def order(t):
        near = (t + 1) // 2
        return jnp.where(lax.rem(t, 2) == 1, near, n_z - near)

    def ag_start(t, carry):
        ag_copy(order(t)).start()
        return carry

    lax.fori_loop(1, n_z, ag_start, 0)
    sib_copy(z).start()

    pair_copy.wait()

    def widen(n, carry):
        raw_ref[pl.ds(pl.multiple_of(n * 512, 512), 512), :] = (
            pair_ref[pl.ds(n * 8, 8)].astype(F32).reshape(512, C)
        )
        return carry

    lax.fori_loop(0, 16, widen, 0)
    wbt = wbt_ref[...]
    wbt_wide = jnp.concatenate([wbt, wbt], axis=1)

    def pair_forward(j, carry):
        normed, inv = norm(raw_ref[pl.ds(j, 128, stride=64), :])
        nrm_ref[j] = normed
        inv_ref[j] = jnp.broadcast_to(inv, (128, C))
        high, low = split(normed)
        both = jnp.concatenate([high, low], axis=1)
        bias_ref[pl.ds(j, H, stride=64), :] = dot_nt(wbt_wide, both)
        return carry

    def gather_step(t, carry):
        lax.fori_loop(t * 8, t * 8 + 8, pair_forward, 0)

        @pl.when(t > 0)
        def _():
            zz = lax.rem(z + n_z - order(t), n_z)
            ag_wait(zz).wait_recv()
            sib_copy(zz).start()

        return carry

    lax.fori_loop(0, n_z, gather_step, 0)

    def sib_arrive(zz, carry):
        sib_wait(zz).wait_recv()
        return carry

    lax.fori_loop(0, n_z, sib_arrive, 0)

    def blocks(ref, s, g):
        one = ref[s, :, g * GW : (g + 1) * GW]
        return jnp.concatenate([one] * GROUP, axis=0) * bdm_ref[...]

    def forward(s, carry):
        keep = jnp.broadcast_to(keep_ref[...][None], (GROUP, 64, 128)) > 0.5
        for g in range(NG):
            sg = s * NG + g
            key_b = blocks(k_ref, s, g)
            value_b = blocks(v_ref, s, g)
            query = qg_ref[s, 0, :, g * GW : (g + 1) * GW]
            gout = qg_ref[s, 1, :, g * GW : (g + 1) * GW]
            scores = dot_nt(key_b, query) * scale + bias_ref[g * 256 : (g + 1) * 256, :]
            scores = jnp.where(keep, scores.reshape(GROUP, 64, 128), NEG)
            top = jnp.max(scores, axis=1)
            expo = jnp.exp(scores - top[:, None, :])
            expo_b = expo.astype(BF)
            pre = dot_nt(value_b, gout).reshape(GROUP, 64, 128)
            st_ref[sg, 0:4, :] = top
            st_ref[sg, 4:8, :] = jnp.sum(expo, axis=1)
            st_ref[sg, 8:12, :] = jnp.sum(expo_b.astype(F32) * pre, axis=1)
            st_ref[sg, 12:16, :] = top
            e_ref[sg] = expo.reshape(256, 128)
            dp_ref[sg] = pre.reshape(256, 128)
            ot_ref[s, g * GW : (g + 1) * GW, :] = dot_tn(value_b, expo_b.reshape(256, 128))
        return carry

    lax.fori_loop(0, 4, forward, 0)

    def b_copy(d):
        c = lax.rem(col + d, n_col)
        return remote(st_ref.at[c], str_ref.at[col], b_send.at[d], b_recv.at[col], at_col(c))

    def b_wait(d):
        c = lax.rem(col + n_col - d, n_col)
        return remote(st_ref.at[c], str_ref.at[c], b_send.at[d], b_recv.at[c], at_col(c))

    def b2_copy(d):
        c = lax.rem(col + d, n_col)
        return remote(res_ref, resr_ref.at[col], b2_send.at[d], b2_recv.at[col], at_col(c))

    def b2_wait(d):
        c = lax.rem(col + n_col - d, n_col)
        return remote(res_ref, resr_ref.at[c], b2_send.at[d], b2_recv.at[c], at_col(c))

    def start_all(make, count):
        def step(d, carry):
            make(d).start()
            return carry

        lax.fori_loop(1, count, step, 0)

    def recv_all(make, count):
        def step(d, carry):
            make(d).wait_recv()
            return carry

        lax.fori_loop(1, count, step, 0)

    def sent_all(make, count):
        def step(d, carry):
            make(d).wait_send()
            return carry

        lax.fori_loop(1, count, step, 0)

    start_all(b_copy, n_col)
    str_ref[col] = st_ref[col]
    recv_all(b_wait, n_col)
    parts = str_ref[...]
    tops = parts[:, 0:4, :]
    top_all = jnp.max(tops, axis=0)
    weight = jnp.exp(tops - top_all[None])
    inv_total = 1.0 / jnp.sum(parts[:, 4:8, :] * weight, axis=0)
    delta = jnp.sum(parts[:, 8:12, :] * weight, axis=0) * inv_total
    res_ref[0:4, :] = top_all
    res_ref[4:8, :] = inv_total
    res_ref[8:12, :] = delta
    res_ref[12:16, :] = delta
    resr_ref[col] = res_ref[...]
    start_all(b2_copy, n_col)
    recv_all(b2_wait, n_col)

    def e_copy(r):
        start = pl.multiple_of(lax.rem(r, 2) * 32, 32)
        return remote(
            dkv_ref.at[r // 2, :, pl.ds(start, 32), :],
            ekv_ref.at[row],
            e_send.at[r],
            e_recv.at[row],
            at_row(r),
        )

    def e_wait(d):
        r = lax.rem(row + n_row - d, n_row)
        return remote(
            dkv_ref.at[0, :, pl.ds(0, 32), :],
            ekv_ref.at[r],
            e_send.at[r],
            e_recv.at[r],
            at_row(r),
        )

    my_half = pl.multiple_of(core * 64, 64)
    their_half = pl.multiple_of((1 - core) * 64, 64)

    def x_copy(s):
        return remote(
            od_ref.at[s, :, pl.ds(their_half, 64), :],
            ods_ref.at[s],
            x_send.at[s],
            x_recv.at[s],
            sibling,
        )

    gb_ref[...] = jnp.zeros_like(gb_ref)
    lane4 = lax.broadcasted_iota(jnp.int32, (64, GW), 1)

    def diagonal(full):
        picked = full[3 * 64 : 4 * 64]
        for h in (2, 1, 0):
            picked = jnp.where(lane4 < (h + 1) * CH, full[h * 64 : (h + 1) * 64], picked)
        return picked

    def backward(t, carry):
        s = lax.rem(t + rest_row, 4)
        keys, values, queries, outs = [], [], [], []
        for g in range(NG):
            sg = s * NG + g
            factor = jnp.exp(st_ref[sg, 0:4, :] - resr_ref[sg, 0:4, :]) * resr_ref[sg, 4:8, :]
            down = resr_ref[sg, 8:12, :]
            probs = e_ref[sg].reshape(GROUP, 64, 128) * factor[:, None, :]
            grads = probs * (dp_ref[sg].reshape(GROUP, 64, 128) - down[:, None, :])
            grads = grads.reshape(256, 128)
            gb_ref[g] += grads
            grads_b = grads.astype(BF)
            probs_b = probs.reshape(256, 128).astype(BF)
            query = qg_ref[s, 0, :, g * GW : (g + 1) * GW]
            gout = qg_ref[s, 1, :, g * GW : (g + 1) * GW]
            keys.append(diagonal(dot_nn(grads_b, query)) * scale)
            values.append(diagonal(dot_nn(probs_b, gout)))
            queries.append(dot_tn(grads_b, blocks(k_ref, s, g)) * scale)
            part = ot_ref[s, g * GW : (g + 1) * GW, :].reshape(GROUP, CH, 128)
            outs.append((part * factor[:, None, :]).reshape(GW, 128).T)
        dkv_ref[s, 0] = jnp.concatenate(keys, axis=1)
        dkv_ref[s, 1] = jnp.concatenate(values, axis=1)
        od_ref[s, 0] = jnp.concatenate(outs, axis=1)
        od_ref[s, 1] = jnp.concatenate(queries, axis=1)
        x_copy(s).start()
        for half in range(2):
            r = s * 2 + half

            @pl.when(r != row)
            def _():
                e_copy(r).start()

        return carry

    lax.fori_loop(0, 4, backward, 0)

    bias_copy = remote(gb_ref, gbr_ref, f_sem.at[0], f_sem.at[1], other_samp)
    bias_copy.start()

    def d_copy(zz):
        rows = pl.ds(pl.multiple_of(lax.rem(zz, 2) * 32, 32), 32)
        return remote(
            dqs_ref.at[zz // 2, rows, :],
            dqr_ref.at[z],
            d_send.at[zz],
            d_recv.at[z],
            at_col(zz * 2 + core),
        )

    def o_copy(zz):
        rows = pl.ds(pl.multiple_of(lax.rem(zz, 2) * 32, 32), 32)
        return remote(
            os_ref.at[zz // 2, rows, :],
            or_ref.at[z],
            o_send.at[zz],
            o_recv.at[z],
            at_col(zz * 2 + core),
        )

    def zz_wait(make_dst, sem_send, sem_recv):
        def make(d):
            zz = lax.rem(z + n_z - d, n_z)
            return remote(
                make_dst.at[zz], make_dst.at[zz], sem_send.at[zz], sem_recv.at[zz], sibling
            )

        return make

    def spread(t, carry):
        s = lax.rem(t + rest_row, 4)
        x_copy(s).wait_recv()
        os_ref[s] = (od_ref[s, 0, pl.ds(my_half, 64), :] + ods_ref[s, 0]).astype(BF)
        dqs_ref[s] = od_ref[s, 1, pl.ds(my_half, 64), :] + ods_ref[s, 1]
        for half in range(2):
            zz = s * 2 + half

            @pl.when(zz != z)
            def _():
                d_copy(zz).start()
                o_copy(zz).start()

        return carry

    lax.fori_loop(0, 4, spread, 0)
    z_rows = pl.ds(pl.multiple_of(lax.rem(z, 2) * 32, 32), 32)
    dqr_ref[z] = dqs_ref[z // 2, z_rows, :]
    or_ref[z] = os_ref[z // 2, z_rows, :]

    bias_copy.wait_recv()
    wg_acc_ref[...] = jnp.zeros_like(wg_acc_ref)
    wbt_tall = jnp.concatenate([wbt, wbt], axis=0)
    pair_scale = total_tokens / samples

    def pair_backward(j, carry):
        grad = bias_ref[pl.ds(j, H, stride=64), :]
        high, low = split(grad)
        grad_hl = jnp.concatenate([high, low], axis=0)
        normed = nrm_ref[j]
        n_high, n_low = split(normed)
        wg_acc_ref[...] += dot_nn(grad_hl, jnp.concatenate([n_high, n_low], axis=1))
        back = norm_back(dot_tn(grad_hl, wbt_tall), normed, inv_ref[j])
        raw_ref[pl.ds(j, 128, stride=64), :] = back * pair_scale
        return carry

    bias_ref[...] = gb_ref[...].reshape(H * 64, 128) + gbr_ref[...].reshape(H * 64, 128)
    lax.fori_loop(0, 64, pair_backward, 0)

    def weight_copy(d):
        c = lax.rem(col + d, n_col)
        return remote(hs_ref.at[0], hr_ref.at[col], h_send.at[d], h_recv.at[col], at_col(c))

    def weight_wait(d):
        c = lax.rem(col + n_col - d, n_col)
        return remote(hs_ref.at[0], hr_ref.at[c], h_send.at[d], h_recv.at[c], at_col(c))

    acc = wg_acc_ref[...]
    hs_ref[0] = (acc[0:H, 0:C] + acc[H:, 0:C]) + (acc[0:H, C:] + acc[H:, C:])
    start_all(weight_copy, n_col)
    hr_ref[col] = hs_ref[0]

    recv_all(zz_wait(dqr_ref, d_send, d_recv), n_z)
    recv_all(zz_wait(or_ref, o_send, o_recv), n_z)
    pm_ref[0] = jnp.sum(or_ref[...].astype(F32), axis=0)
    pm_ref[1] = jnp.sum(dqr_ref[...], axis=0)
    pm_copy = remote(pm_ref, pmr_ref, pm_sem.at[0], pm_sem.at[1], swapped)
    pm_own = pltpu.make_async_copy(pm_ref, pmr_ref, pm_sem.at[2])

    @pl.when(jnp.logical_not(is_diag))
    def _():
        pm_copy.start()

    @pl.when(is_diag)
    def _():
        pm_own.start()

    def narrow(n, carry):
        pair_ref[pl.ds(n * 8, 8)] = (
            raw_ref[pl.ds(pl.multiple_of(n * 512, 512), 512), :].reshape(8, 64, C).astype(BF)
        )
        return carry

    lax.fori_loop(0, 16, narrow, 0)
    out_copy = pltpu.make_async_copy(pair_ref, pg_hbm, out_sem)
    out_copy.start()

    recv_all(weight_wait, n_col)
    hs_ref[1] = jnp.sum(hr_ref[...], axis=0)

    def weight2_copy(d):
        r = lax.rem(row + d, n_row)
        return remote(hs_ref.at[1], hr2_ref.at[row], h2_send.at[d], h2_recv.at[row], at_row(r))

    def weight2_wait(d):
        r = lax.rem(row + n_row - d, n_row)
        return remote(hs_ref.at[1], hr2_ref.at[r], h2_send.at[d], h2_recv.at[r], at_row(r))

    start_all(weight2_copy, n_row)
    hr2_ref[row] = hs_ref[1]

    ekv_ref[row] = dkv_ref[rest_row, :, own_rows, :]
    recv_all(e_wait, n_row)
    grad_kv = jnp.sum(ekv_ref[...], axis=0)

    def back_project(grad, weight_ref):
        high, low = split(grad)
        both = dot_nt(jnp.concatenate([high, low], axis=0), weight_ref[...])
        return both[0:32] + both[32:64]

    total = back_project(grad_kv[0], wk_ref) + back_project(grad_kv[1], wv_ref)

    @pl.when(jnp.logical_not(is_diag))
    def _():
        pm_copy.wait()

    @pl.when(is_diag)
    def _():
        pm_own.wait()

    total = total + back_project(pmr_ref[1], wq_ref)
    own_sig = sig_ref[...]
    cot = cot_ref[rest_row, own_rows, :].astype(F32)
    grad_gate = (cot * pmr_ref[0] * own_sig * (1.0 - own_sig)).astype(BF)
    total = total + dot_nt(grad_gate, wg_ref[...])
    own_normed, own_inv = norm(tok_ref[rest_row, own_rows, :].astype(F32) + emb_ref[own_rows, :])
    tg_ref[rest_row, own_rows, :] = norm_back(total, own_normed, own_inv).astype(BF)

    def g_copy(d):
        r = lax.rem(row + d, n_row)
        mine = tg_ref.at[rest_row, own_rows, :]
        return remote(mine, mine, g_send.at[d], g_recv.at[row], at_row(r))

    def g_wait(d):
        r = lax.rem(row + n_row - d, n_row)
        start = pl.multiple_of(lax.rem(r, 2) * 32, 32)
        theirs = tg_ref.at[r // 2, pl.ds(start, 32), :]
        return remote(theirs, theirs, g_send.at[d], g_recv.at[r], at_row(r))

    start_all(g_copy, n_row)
    recv_all(weight2_wait, n_row)
    bw_ref[...] = jnp.sum(hr2_ref[...], axis=0) * (1.0 / samples)

    sent_all(ag_copy, n_z)
    sent_all(b_copy, n_col)
    sent_all(b2_copy, n_col)
    sent_all(weight_copy, n_col)
    sent_all(weight2_copy, n_row)
    bias_copy.wait_send()

    def left(n, carry):
        sib_copy(n).wait_send()

        @pl.when(n != row)
        def _():
            e_copy(n).wait_send()

        @pl.when(n != z)
        def _():
            d_copy(n).wait_send()
            o_copy(n).wait_send()

        return carry

    lax.fori_loop(0, n_z, left, 0)

    def left_x(s, carry):
        x_copy(s).wait_send()
        return carry

    lax.fori_loop(0, 4, left_x, 0)
    recv_all(g_wait, n_row)
    sent_all(g_copy, n_row)
    out_copy.wait()


def body(
    tokens, restype, type_table, key_mask, pair, w_bias, w_query, w_key, w_value, w_gate, cotangent
):
    n_row = lax.axis_size("row")
    n_col = lax.axis_size("col")
    n_z = n_col // 2
    samples = tokens.shape[0] * lax.axis_size("samp")
    total_tokens = tokens.shape[1] * n_col
    vmem = pl.BlockSpec(memory_space=pltpu.VMEM)
    hbm = pl.BlockSpec(memory_space=pl.ANY)
    dma = pltpu.SemaphoreType.DMA
    token_grad, weight_grad, pair_grad = pl.pallas_call(
        functools.partial(kernel, (n_row, n_col, total_tokens, samples)),
        out_shape=(
            jax.ShapeDtypeStruct((4, 64, D), BF),
            jax.ShapeDtypeStruct((H, C), F32),
            jax.ShapeDtypeStruct((128, 64, C), BF),
        ),
        in_specs=[vmem] * 6 + [hbm] * 5,
        out_specs=(vmem, vmem, hbm),
        scratch_shapes=[
            pltpu.VMEM((D, D), BF),
            pltpu.VMEM((D, D), BF),
            pltpu.VMEM((D, D), BF),
            pltpu.VMEM((D, D), BF),
            pltpu.VMEM((128, 64, C), BF),
            pltpu.VMEM((8192, C), F32),
            pltpu.VMEM((64, 128, C), F32),
            pltpu.VMEM((64, 128, C), F32),
            pltpu.VMEM((H * 64, 128), F32),
            pltpu.VMEM((64, D), F32),
            pltpu.VMEM((16, 128), F32),
            pltpu.VMEM((4, 64, D), BF),
            pltpu.VMEM((4, 64, D), BF),
            pltpu.VMEM((32, D), F32),
            pltpu.VMEM((2, 32, D), BF),
            pltpu.VMEM((4, 2, 128, D), BF),
            pltpu.VMEM((256, GW), BF),
            pltpu.VMEM((64, 128), F32),
            pltpu.VMEM((16, 256, 128), F32),
            pltpu.VMEM((16, 256, 128), F32),
            pltpu.VMEM((4, D, 128), F32),
            pltpu.VMEM((16, 16, 128), F32),
            pltpu.VMEM((16, 16, 128), F32),
            pltpu.VMEM((16, 128), F32),
            pltpu.VMEM((16, 16, 128), F32),
            pltpu.VMEM((NG, 256, 128), F32),
            pltpu.VMEM((NG, 256, 128), F32),
            pltpu.VMEM((4, 2, 64, D), F32),
            pltpu.VMEM((n_row, 2, 32, D), F32),
            pltpu.VMEM((4, 2, 128, D), F32),
            pltpu.VMEM((4, 2, 64, D), F32),
            pltpu.VMEM((4, 64, D), F32),
            pltpu.VMEM((n_z, 32, D), F32),
            pltpu.VMEM((4, 64, D), BF),
            pltpu.VMEM((n_z, 32, D), BF),
            pltpu.VMEM((2, 32, D), F32),
            pltpu.VMEM((2, 32, D), F32),
            pltpu.VMEM((2 * H, 2 * C), F32),
            pltpu.VMEM((n_col, H, C), F32),
            pltpu.VMEM((2, H, C), F32),
            pltpu.VMEM((n_row, H, C), F32),
            dma((4,)),
            dma,
            dma,
            dma((3,)),
            dma((n_z,)),
            dma((n_z,)),
            dma((n_z,)),
            dma((n_z,)),
            dma((n_col,)),
            dma((n_col,)),
            dma((n_col,)),
            dma((n_col,)),
            dma((n_row,)),
            dma((n_row,)),
            dma((4,)),
            dma((4,)),
            dma((n_z,)),
            dma((n_z,)),
            dma((n_z,)),
            dma((n_z,)),
            dma((2,)),
            dma((3,)),
            dma((n_row,)),
            dma((n_row,)),
            dma((n_col,)),
            dma((n_col,)),
            dma((n_row,)),
            dma((n_row,)),
        ],
        compiler_params=pltpu.CompilerParams(
            collective_id=0, has_side_effects=True, vmem_limit_bytes=60 * 1024 * 1024
        ),
    )(
        tokens,
        restype.reshape(64, 1),
        type_table,
        key_mask.reshape(64, 1),
        w_bias.T,
        cotangent,
        w_query,
        w_key,
        w_value,
        w_gate,
        pair,
    )
    return (token_grad, pair_grad, weight_grad.T)


def solution(mesh):
    placed = (
        P("samp", "col", None),
        P("col"),
        P(),
        P("col"),
        P("row", "col", None),
        P(),
        P(),
        P(),
        P(),
        P(),
        P("samp", "col", None),
    )
    return jax.shard_map(
        body,
        mesh=mesh,
        in_specs=placed,
        out_specs=(P("samp", "col", None), P("row", "col", None), P()),
        check_vma=False,
    )
```

```python
import functools
import math

import jax
import jax.numpy as jnp
from jax import lax
from jax.experimental import pallas as pl
from jax.experimental.pallas import tpu as pltpu
from jax.sharding import PartitionSpec as P

D = 768
H = 16
CH = 48
C = 128
NTYPE = 32
GROUP = 4
NG = H // GROUP
GW = GROUP * CH
EPS = 1e-05
NEG = -1000000000.0
BF = jnp.bfloat16
F32 = jnp.float32
MESH = pl.DeviceIdType.MESH


def dot_nn(a, b):
    return jnp.dot(a, b, preferred_element_type=F32)


def dot_nt(a, b):
    return lax.dot_general(a, b, (((1,), (1,)), ((), ())), preferred_element_type=F32)


def dot_tn(a, b):
    return lax.dot_general(a, b, (((0,), (0,)), ((), ())), preferred_element_type=F32)


def split(x):
    high = x.astype(BF)
    return high, (x - high.astype(F32)).astype(BF)


def norm(x):
    centred = x - jnp.mean(x, axis=-1, keepdims=True)
    inv = lax.rsqrt(jnp.mean(centred * centred, axis=-1, keepdims=True) + EPS)
    return centred * inv, inv


def norm_back(grad, normed, inv):
    return inv * (
        grad
        - jnp.mean(grad, axis=-1, keepdims=True)
        - normed * jnp.mean(grad * normed, axis=-1, keepdims=True)
    )


def kernel(
    sizes,
    tok_ref,
    rest_ref,
    table_ref,
    mask_ref,
    wbt_ref,
    cot_ref,
    wq_hbm,
    wk_hbm,
    wv_hbm,
    wg_hbm,
    pair_hbm,
    tg_ref,
    bw_ref,
    pg_ref,
    wq_ref,
    wk_ref,
    wv_ref,
    wg_ref,
    pair_ref,
    raw_ref,
    nrm_ref,
    inv_ref,
    bias_ref,
    emb_ref,
    k_ref,
    v_ref,
    sig_ref,
    qgs_ref,
    qg_ref,
    bdm_ref,
    keep_ref,
    e_ref,
    dp_ref,
    ot_ref,
    st_ref,
    str_ref,
    res_ref,
    resr_ref,
    gbs_ref,
    gbr_ref,
    gr_ref,
    pr_ref,
    dkv_ref,
    ekv_ref,
    ey_ref,
    od_ref,
    ods_ref,
    dqs_ref,
    dqr_ref,
    pm_ref,
    pmr_ref,
    inner_ref,
    hr_ref,
    hs_ref,
    hr2_ref,
    w_sem,
    pair_sem,
    t_sem,
    ag_send,
    ag_recv,
    sib_send,
    sib_recv,
    b_send,
    b_recv,
    b2_send,
    b2_recv,
    e_send,
    e_recv,
    ey_sem,
    x_send,
    x_recv,
    d_send,
    d_recv,
    f_send,
    f_recv,
    pm_sem,
    g_send,
    g_recv,
    h_send,
    h_recv,
    h2_send,
    h2_recv,
):
    n_row, n_col, total_tokens, samples = sizes
    samp = lax.axis_index("samp")
    row = lax.axis_index("row")
    col = lax.axis_index("col")
    core = lax.rem(col, 2)
    z = col // 2
    n_z = n_col // 2
    scale = 1.0 / math.sqrt(CH)
    rest_row = row // 2
    own_tok = pl.multiple_of(lax.rem(row, 2) * 32, 32)

    def at_col(c):
        return (samp, row, c)

    def at_row(r):
        return (samp, r, col)

    sibling = at_col(z * 2 + 1 - core)

    def differ(a, b):
        return sum(lax.rem(a // bit + b // bit, 2) * bit for bit in (1, 2, 4))

    slice_here = differ(z, row)
    query_dev = (samp, z, slice_here * 2 + core)
    owner_dev = (samp, slice_here, row * 2 + core)
    is_self = row + z == 0
    other_samp = (1 - samp, row, col)

    def remote(src, dst, send, recv, device):
        return pltpu.make_async_remote_copy(
            src_ref=src,
            dst_ref=dst,
            send_sem=send,
            recv_sem=recv,
            device_id=device,
            device_id_type=MESH,
        )

    weights = [
        pltpu.make_async_copy(src, dst, w_sem.at[n])
        for n, (src, dst) in enumerate(
            ((wq_hbm, wq_ref), (wg_hbm, wg_ref), (wk_hbm, wk_ref), (wv_hbm, wv_ref))
        )
    ]
    for copy in weights:
        copy.start()
    pair_copy = pltpu.make_async_copy(pair_hbm, pair_ref, pair_sem)
    pair_copy.start()

    barrier = pltpu.get_barrier_semaphore()

    def greet(device):
        pl.semaphore_signal(barrier, inc=1, device_id=device, device_id_type=MESH)

    def greet_col(d, carry):
        greet(at_col(lax.rem(col + d, n_col)))
        return carry

    def greet_row(d, carry):
        greet(at_row(lax.rem(row + d, n_row)))
        return carry

    lax.fori_loop(1, n_col, greet_col, 0)
    lax.fori_loop(1, n_row, greet_row, 0)
    greet(other_samp)

    @pl.when(jnp.logical_not(is_self))
    def _():
        greet(query_dev)
        greet(owner_dev)

    onehot = jnp.where(rest_ref[...] == lax.broadcasted_iota(jnp.int32, (NTYPE, 64), 0), 1.0, 0.0)
    emb_ref[...] = dot_tn(onehot.astype(BF), table_ref[...])
    own_rows = pl.ds(own_tok, 32)
    own_normed, own_inv = norm(tok_ref[rest_row, own_rows, :].astype(F32) + emb_ref[own_rows, :])
    own_act = own_normed.astype(BF)
    weights[0].wait()
    qgs_ref[0] = dot_nn(own_act, wq_ref[...]).astype(BF)
    weights[1].wait()
    gate = dot_nn(own_act, wg_ref[...]).astype(BF).astype(F32)
    sig = jax.nn.sigmoid(gate)
    sig_ref[...] = sig
    own_cot = cot_ref[rest_row, own_rows, :].astype(F32)
    qgs_ref[1] = (own_cot * sig).astype(BF)

    weights[2].wait()
    weights[3].wait()

    def project(s, carry):
        normed, _ = norm(tok_ref[s].astype(F32) + emb_ref[...])
        act = normed.astype(BF)
        k_ref[s] = dot_nn(act, wk_ref[...]).astype(BF)
        v_ref[s] = dot_nn(act, wv_ref[...]).astype(BF)
        return carry

    lax.fori_loop(0, 4, project, 0)
    lane = lax.broadcasted_iota(jnp.int32, (64, GW), 1)
    for h in range(GROUP):
        inside = jnp.logical_and(lane >= h * CH, lane < (h + 1) * CH)
        bdm_ref[h * 64 : (h + 1) * 64, :] = jnp.where(inside, 1.0, 0.0).astype(BF)
    first_row = lax.broadcasted_iota(jnp.int32, (16, 64), 0) == 0
    kept = jnp.where(jnp.logical_and(mask_ref[...] == 1, first_row), 1.0, 0.0)
    keep_ref[...] = dot_tn(kept.astype(BF), jnp.ones((16, 128), BF))

    pair_copy.wait()

    def widen(n, carry):
        raw_ref[pl.ds(pl.multiple_of(n * 512, 512), 512), :] = (
            pair_ref[pl.ds(n * 8, 8)].astype(F32).reshape(512, C)
        )
        return carry

    lax.fori_loop(0, 16, widen, 0)
    @pl.when(is_self)
    def _():
        pl.semaphore_wait(barrier, n_col + n_row - 1)

    @pl.when(jnp.logical_not(is_self))
    def _():
        pl.semaphore_wait(barrier, n_col + n_row + 1)

    def region(number):
        start = pl.multiple_of(core * 64 + lax.rem(number, 2) * 32, 32)
        return qg_ref.at[number // 2, :, pl.ds(start, 32), :]

    to_swapped = remote(qgs_ref, region(row), t_sem.at[0], t_sem.at[1], query_dev)
    from_swapped = remote(qgs_ref, region(slice_here), t_sem.at[0], t_sem.at[1], owner_dev)
    keep_own = pltpu.make_async_copy(qgs_ref, region(slice_here), t_sem.at[2])

    @pl.when(jnp.logical_not(is_self))
    def _():
        to_swapped.start()

    @pl.when(is_self)
    def _():
        keep_own.start()

    @pl.when(jnp.logical_not(is_self))
    def _():
        to_swapped.wait_send()
        from_swapped.wait_recv()

    @pl.when(is_self)
    def _():
        keep_own.wait()

    def part_of(zz, kk, part):
        number = differ(zz, row)
        start = pl.multiple_of(kk * 64 + lax.rem(number, 2) * 32, 32)
        return qg_ref.at[number // 2, part, pl.ds(start, 32), :]

    def ag_copy(way, part, step):
        origin = lax.rem(z + n_z - way * step, n_z)
        mine = part_of(origin, core, part)
        sem = (part * 2 + (way + 1) // 2) * 4 + step
        there = at_col(lax.rem(z + n_z + way, n_z) * 2 + core)
        return remote(mine, mine, ag_send.at[sem], ag_recv.at[sem], there)

    def ag_wait(way, part, step):
        origin = lax.rem(z + 2 * n_z - way * (step + 1), n_z)
        mine = part_of(origin, core, part)
        sem = (part * 2 + (way + 1) // 2) * 4 + step
        return remote(mine, mine, ag_send.at[sem], ag_recv.at[sem], sibling)

    def sib_copy(zz, part):
        mine = part_of(zz, core, part)
        sem = zz * 2 + part
        return remote(mine, mine, sib_send.at[sem], sib_recv.at[sem], sibling)

    def sib_wait(zz, part):
        theirs = part_of(zz, 1 - core, part)
        sem = zz * 2 + part
        return remote(theirs, theirs, sib_send.at[sem], sib_recv.at[sem], sibling)

    def last_step(way, part):
        return 3 if (way == 1) == (part == 0) else 2

    for part in range(2):
        for way in (1, -1):
            ag_copy(way, part, 0).start()
        sib_copy(z, part).start()

    wbt = wbt_ref[...]
    wbt_wide = jnp.concatenate([wbt, wbt], axis=1)
    mean_one = jnp.full((C, C), 1.0 / C, BF)
    mean_two = jnp.full((2 * C, C), 1.0 / C, BF)

    def pair_forward(n, carry):
        first = n * 4
        values = jnp.concatenate(
            [raw_ref[pl.ds(first + u, 128, stride=64), :] for u in range(4)], axis=0
        )
        centred = values - dot_nn(values.astype(BF), mean_one)
        variance = dot_nn(jnp.concatenate(split(centred * centred), axis=1), mean_two)
        inv = lax.rsqrt(variance + EPS)
        normed = centred * inv
        nrm_ref[pl.ds(first, 4)] = normed.reshape(4, 128, C)
        inv_ref[pl.ds(first, 4)] = inv.reshape(4, 128, C)
        both = jnp.concatenate(split(normed), axis=1)
        for u in range(4):
            bias_ref[pl.ds(first + u, H, stride=64), :] = dot_nt(
                wbt_wide, both[u * 128 : (u + 1) * 128]
            )
        return carry

    def gather_step(step, carry):
        for part in range(2):
            for n in range(2):
                pair_forward(step * 4 + part * 2 + n, 0)
            for way in (1, -1):

                @pl.when(step <= last_step(way, part))
                def _():
                    ag_wait(way, part, step).wait_recv()

                @pl.when(step < last_step(way, part))
                def _():
                    ag_copy(way, part, step + 1).start()

                @pl.when(step <= last_step(way, part))
                def _():
                    sib_copy(lax.rem(z + 2 * n_z - way * (step + 1), n_z), part).start()

        return carry

    lax.fori_loop(0, 4, gather_step, 0)

    def sib_arrive(zz, carry):
        for part in range(2):
            sib_wait(zz, part).wait_recv()
        return carry

    lax.fori_loop(0, n_z, sib_arrive, 0)

    def blocks(ref, s, g):
        one = ref[s, :, g * GW : (g + 1) * GW]
        return jnp.concatenate([one] * GROUP, axis=0) * bdm_ref[...]

    def forward(s, carry):
        keep = jnp.broadcast_to(keep_ref[...][None], (GROUP, 64, 128)) > 0.5
        for g in range(NG):
            sg = s * NG + g
            key_b = blocks(k_ref, s, g)
            value_b = blocks(v_ref, s, g)
            query = qg_ref[s, 0, :, g * GW : (g + 1) * GW]
            gout = qg_ref[s, 1, :, g * GW : (g + 1) * GW]
            scores = dot_nt(key_b, query) * scale + bias_ref[g * 256 : (g + 1) * 256, :]
            scores = jnp.where(keep, scores.reshape(GROUP, 64, 128), NEG)
            top = jnp.max(scores, axis=1)
            expo = jnp.exp(scores - top[:, None, :])
            expo_b = expo.astype(BF)
            pre = dot_nt(value_b, gout).reshape(GROUP, 64, 128)
            st_ref[sg, 0:4, :] = top
            st_ref[sg, 4:8, :] = jnp.sum(expo, axis=1)
            st_ref[sg, 8:12, :] = jnp.sum(expo_b.astype(F32) * pre, axis=1)
            st_ref[sg, 12:16, :] = top
            e_ref[sg] = expo.reshape(256, 128)
            dp_ref[sg] = pre.reshape(256, 128)
            ot_ref[s, g * GW : (g + 1) * GW, :] = dot_tn(value_b, expo_b.reshape(256, 128))
        return carry

    lax.fori_loop(0, 4, forward, 0)

    def b_copy(d):
        c = lax.rem(col + d, n_col)
        return remote(st_ref.at[c], str_ref.at[col], b_send.at[d], b_recv.at[col], at_col(c))

    def b_wait(d):
        c = lax.rem(col + n_col - d, n_col)
        return remote(st_ref.at[c], str_ref.at[c], b_send.at[d], b_recv.at[c], at_col(c))

    def b2_copy(d):
        c = lax.rem(col + d, n_col)
        return remote(res_ref, resr_ref.at[col], b2_send.at[d], b2_recv.at[col], at_col(c))

    def b2_wait(d):
        c = lax.rem(col + n_col - d, n_col)
        return remote(res_ref, resr_ref.at[c], b2_send.at[d], b2_recv.at[c], at_col(c))

    def start_all(make, count):
        def step(d, carry):
            make(d).start()
            return carry

        lax.fori_loop(1, count, step, 0)

    def recv_all(make, count):
        def step(d, carry):
            make(d).wait_recv()
            return carry

        lax.fori_loop(1, count, step, 0)

    def sent_all(make, count):
        def step(d, carry):
            make(d).wait_send()
            return carry

        lax.fori_loop(1, count, step, 0)

    start_all(b_copy, n_col)
    str_ref[col] = st_ref[col]
    recv_all(b_wait, n_col)
    parts = str_ref[...]
    tops = parts[:, 0:4, :]
    top_all = jnp.max(tops, axis=0)
    weight = jnp.exp(tops - top_all[None])
    inv_total = 1.0 / jnp.sum(parts[:, 4:8, :] * weight, axis=0)
    delta = jnp.sum(parts[:, 8:12, :] * weight, axis=0) * inv_total
    res_ref[0:4, :] = top_all
    res_ref[4:8, :] = inv_total
    res_ref[8:12, :] = delta
    res_ref[12:16, :] = delta
    resr_ref[col] = res_ref[...]
    start_all(b2_copy, n_col)
    recv_all(b2_wait, n_col)

    def e_copy(r):
        start = pl.multiple_of(lax.rem(r, 2) * 32, 32)
        return remote(
            dkv_ref.at[r // 2, pl.ds(start, 32), :],
            ekv_ref.at[r // 4, lax.rem(row, 4)],
            e_send.at[r],
            e_recv.at[(r // 4) * 4 + lax.rem(row, 4)],
            at_row((row // 4) * 4 + lax.rem(r, 4)),
        )

    def e_wait(hi, d):
        x = lax.rem(row + 4 - d, 4)
        return remote(
            dkv_ref.at[0, pl.ds(0, 32), :],
            ekv_ref.at[hi, x],
            e_send.at[hi * 4 + x],
            e_recv.at[hi * 4 + x],
            at_row((row // 4) * 4 + x),
        )

    def e_sum(hi):
        for d in range(1, 4):
            e_wait(hi, d).wait_recv()
        r = hi * 4 + lax.rem(row, 4)
        start = pl.multiple_of(lax.rem(r, 2) * 32, 32)
        ekv_ref[hi, lax.rem(row, 4)] = dkv_ref[r // 2, pl.ds(start, 32), :]
        return jnp.sum(ekv_ref[hi], axis=0)

    my_half = pl.multiple_of(core * 64, 64)
    their_half = pl.multiple_of((1 - core) * 64, 64)

    def x_copy(s):
        return remote(
            od_ref.at[s, :, pl.ds(their_half, 64), :],
            ods_ref.at[s],
            x_send.at[s],
            x_recv.at[s],
            sibling,
        )

    lane4 = lax.broadcasted_iota(jnp.int32, (64, GW), 1)

    def diagonal(full):
        picked = full[3 * 64 : 4 * 64]
        for h in (2, 1, 0):
            picked = jnp.where(lane4 < (h + 1) * CH, full[h * 64 : (h + 1) * 64], picked)
        return picked

    def factor_of(sg):
        return jnp.exp(st_ref[sg, 0:4, :] - resr_ref[sg, 0:4, :]) * resr_ref[sg, 4:8, :]

    def bias_copy(g):
        return remote(gbs_ref.at[g], gbr_ref.at[g], f_send.at[g], f_recv.at[g], other_samp)

    def score_grads(g, carry):
        total = jnp.zeros((256, 128), F32)
        for s in range(4):
            sg = s * NG + g
            factor = factor_of(sg)
            down = resr_ref[sg, 8:12, :]
            probs = e_ref[sg].reshape(GROUP, 64, 128) * factor[:, None, :]
            grads = probs * (dp_ref[sg].reshape(GROUP, 64, 128) - down[:, None, :])
            grads = grads.reshape(256, 128)
            total = total + grads
            gr_ref[sg] = grads.astype(BF)
            pr_ref[sg] = probs.reshape(256, 128).astype(BF)
        gbs_ref[g] = total
        bias_copy(g).start()
        return carry

    lax.fori_loop(0, NG, score_grads, 0)

    def query_side(t, carry):
        s = lax.rem(t + rest_row, 4)
        outs, queries = [], []
        for g in range(NG):
            sg = s * NG + g
            part = ot_ref[s, g * GW : (g + 1) * GW, :].reshape(GROUP, CH, 128)
            outs.append((part * factor_of(sg)[:, None, :]).reshape(GW, 128).T)
            queries.append(dot_tn(gr_ref[sg], blocks(k_ref, s, g)) * scale)
        od_ref[s, 0] = jnp.concatenate(outs, axis=1)
        od_ref[s, 1] = jnp.concatenate(queries, axis=1)
        x_copy(s).start()
        return carry

    lax.fori_loop(0, 4, query_side, 0)

    def add_sibling(t, carry):
        s = lax.rem(t + rest_row, 4)
        x_copy(s).wait_recv()
        dqs_ref[s] = od_ref[s, :, pl.ds(my_half, 64), :] + ods_ref[s]
        return carry

    lax.fori_loop(0, 4, add_sibling, 0)

    def own_part(zz, part):
        number = differ(zz, row)
        start = pl.multiple_of(lax.rem(number, 2) * 32 + part * 16, 16)
        return dqs_ref.at[number // 2, :, pl.ds(start, 16), :]

    def rs_copy(way, part, left, src):
        lane_of = part * 2 + (way + 1) // 2
        sem = lane_of * 4 + left - 1
        there = at_col(lax.rem(z + n_z + way, n_z) * 2 + core)
        return remote(src, dqr_ref.at[lane_of, left - 1], d_send.at[sem], d_recv.at[sem], there)

    def rs_slot(way, part, left):
        return dqr_ref.at[part * 2 + (way + 1) // 2, left - 1]

    def rs_first(way, part):
        return 4 if (way == 1) == (part == 0) else 3

    def rs_pass(way, part, left):
        slot = rs_slot(way, part, left)
        rs_copy(way, part, left, slot).wait_recv()
        slot[...] = slot[...] + own_part(lax.rem(z + 2 * n_z + way * (left - 1), n_z), part)[...]
        rs_copy(way, part, left - 1, slot).start()

    for part in range(2):
        for way in (1, -1):
            first = rs_first(way, part)
            target = lax.rem(z + n_z + way * first, n_z)
            rs_copy(way, part, first, own_part(target, part)).start()

    def ring_step(t):
        for part in range(2):
            for way in (1, -1):
                first = rs_first(way, part)

                @pl.when(t < first - 1)
                def _():
                    rs_pass(way, part, first - t)

    def back_project(grad, weight_ref):
        both = dot_nt(jnp.concatenate(split(grad), axis=0), weight_ref[...])
        half = grad.shape[0]
        return both[0:half] + both[half:]

    def backward(t, carry):
        s = lax.rem(t + rest_row, 4)
        keys, values = [], []
        for g in range(NG):
            sg = s * NG + g
            query = qg_ref[s, 0, :, g * GW : (g + 1) * GW]
            gout = qg_ref[s, 1, :, g * GW : (g + 1) * GW]
            keys.append(diagonal(dot_nn(gr_ref[sg], query)) * scale)
            values.append(diagonal(dot_nn(pr_ref[sg], gout)))
        dkv_ref[s] = back_project(jnp.concatenate(keys, axis=1), wk_ref) + back_project(
            jnp.concatenate(values, axis=1), wv_ref
        )
        for half in range(2):
            r = s * 2 + half

            @pl.when(lax.rem(r, 4) != lax.rem(row, 4))
            def _():
                e_copy(r).start()

        ring_step(t)
        return carry

    lax.fori_loop(0, 4, backward, 0)

    ey_copy = remote(
        ey_ref.at[0], ey_ref.at[1], ey_sem.at[0], ey_sem.at[1], at_row(lax.rem(row + 4, n_row))
    )
    ey_ref[0] = e_sum(1 - row // 4)
    ey_copy.start()

    for part in range(2):
        for way in (1, -1):
            rs_copy(way, part, 1, rs_slot(way, part, 1)).wait_recv()
    for part in range(2):
        pm_ref[:, part * 16 : (part + 1) * 16, :] = (
            own_part(z, part)[...] + rs_slot(1, part, 1)[...] + rs_slot(-1, part, 1)[...]
        )
    pm_copy = remote(pm_ref, pmr_ref, pm_sem.at[0], pm_sem.at[1], owner_dev)
    pm_own = pltpu.make_async_copy(pm_ref, pmr_ref, pm_sem.at[2])

    @pl.when(jnp.logical_not(is_self))
    def _():
        pm_copy.start()

    @pl.when(is_self)
    def _():
        pm_own.start()

    def bias_arrive(g, carry):
        bias_copy(g).wait_recv()
        return carry

    lax.fori_loop(0, NG, bias_arrive, 0)
    summed = (gbs_ref[...] + gbr_ref[...]).reshape(H * 64, 128)
    inner = jnp.sum((summed * bias_ref[...]).reshape(H, 64, 128), axis=0) * (1.0 / C)
    bias_ref[...] = summed
    inner_h = inner.astype(BF).astype(F32)
    inner_l = inner - inner_h
    which = lax.broadcasted_iota(jnp.int32, (64, 16, 128), 1)
    inner_ref[...] = jnp.where(
        which == 0, inner_h[:, None, :], jnp.where(which == 1, inner_l[:, None, :], 0.0)
    ).astype(BF)
    weight = wbt.astype(F32) * (total_tokens / samples)
    weight_h, weight_l = split(weight - jnp.mean(weight, axis=1, keepdims=True))
    blank = jnp.zeros((H, C), BF)
    ones = jnp.full((H, C), total_tokens / samples, BF)
    spread_w = jnp.concatenate(
        [
            jnp.concatenate([weight_h, weight_h, weight_l, blank], axis=0),
            jnp.concatenate([blank, blank, blank, ones], axis=0),
        ],
        axis=1,
    )

    def pair_backward(n, acc):
        grads, normeds = [], []
        for u in range(4):
            j = n * 4 + u
            high, low = split(bias_ref[pl.ds(j, H, stride=64), :])
            both = jnp.concatenate([high, low], axis=0)
            normed = nrm_ref[j]
            wide = dot_tn(jnp.concatenate([both, high, inner_ref[j]], axis=0), spread_w)
            raw_ref[pl.ds(j, 128, stride=64), :] = inv_ref[j] * (
                wide[:, 0:C] - normed * wide[:, C:]
            )
            grads.append(both)
            normeds.append(jnp.concatenate(split(normed), axis=1))
        for u in (0, 2):
            acc = acc + dot_nn(
                jnp.concatenate(grads[u : u + 2], axis=1),
                jnp.concatenate(normeds[u : u + 2], axis=0),
            )
        return acc

    acc = lax.fori_loop(0, 16, pair_backward, jnp.zeros((2 * H, 2 * C), F32))

    def weight_copy(d):
        c = lax.rem(col + d, n_col)
        return remote(hs_ref.at[0], hr_ref.at[col], h_send.at[d], h_recv.at[col], at_col(c))

    def weight_wait(d):
        c = lax.rem(col + n_col - d, n_col)
        return remote(hs_ref.at[0], hr_ref.at[c], h_send.at[d], h_recv.at[c], at_col(c))

    hs_ref[0] = (acc[0:H, 0:C] + acc[H:, 0:C]) + (acc[0:H, C:] + acc[H:, C:])
    start_all(weight_copy, n_col)
    hr_ref[col] = hs_ref[0]

    def narrow(n, carry):
        pg_ref[pl.ds(n * 8, 8)] = (
            raw_ref[pl.ds(pl.multiple_of(n * 512, 512), 512), :].reshape(8, 64, C).astype(BF)
        )
        return carry

    lax.fori_loop(0, 16, narrow, 0)

    recv_all(weight_wait, n_col)
    hs_ref[1] = jnp.sum(hr_ref[...], axis=0)

    def weight2_copy(d):
        r = lax.rem(row + d, n_row)
        return remote(hs_ref.at[1], hr2_ref.at[row], h2_send.at[d], h2_recv.at[row], at_row(r))

    def weight2_wait(d):
        r = lax.rem(row + n_row - d, n_row)
        return remote(hs_ref.at[1], hr2_ref.at[r], h2_send.at[d], h2_recv.at[r], at_row(r))

    start_all(weight2_copy, n_row)
    hr2_ref[row] = hs_ref[1]

    total = e_sum(row // 4)
    ey_copy.wait_recv()
    total = total + ey_ref[1]

    @pl.when(jnp.logical_not(is_self))
    def _():
        pm_copy.wait()

    @pl.when(is_self)
    def _():
        pm_own.wait()

    total = total + back_project(pmr_ref[1], wq_ref)
    own_sig = sig_ref[...]
    cot = cot_ref[rest_row, own_rows, :].astype(F32)
    grad_gate = (cot * pmr_ref[0] * own_sig * (1.0 - own_sig)).astype(BF)
    total = total + dot_nt(grad_gate, wg_ref[...])
    own_normed, own_inv = norm(tok_ref[rest_row, own_rows, :].astype(F32) + emb_ref[own_rows, :])
    tg_ref[rest_row, own_rows, :] = norm_back(total, own_normed, own_inv).astype(BF)

    def g_copy(d):
        r = lax.rem(row + d, n_row)
        mine = tg_ref.at[rest_row, own_rows, :]
        return remote(mine, mine, g_send.at[d], g_recv.at[row], at_row(r))

    def g_wait(d):
        r = lax.rem(row + n_row - d, n_row)
        start = pl.multiple_of(lax.rem(r, 2) * 32, 32)
        theirs = tg_ref.at[r // 2, pl.ds(start, 32), :]
        return remote(theirs, theirs, g_send.at[d], g_recv.at[r], at_row(r))

    start_all(g_copy, n_row)
    recv_all(weight2_wait, n_row)
    bw_ref[...] = jnp.sum(hr2_ref[...], axis=0) * (1.0 / samples)

    sent_all(b_copy, n_col)
    sent_all(b2_copy, n_col)
    sent_all(weight_copy, n_col)
    sent_all(weight2_copy, n_row)
    ey_copy.wait_send()
    for part in range(2):
        for way in (1, -1):

            def left_ag(step, carry):
                ag_copy(way, part, step).wait_send()
                return carry

            lax.fori_loop(0, last_step(way, part) + 1, left_ag, 0)

            def left_rs(left, carry):
                rs_copy(way, part, left, rs_slot(way, part, left)).wait_send()
                return carry

            lax.fori_loop(1, rs_first(way, part) + 1, left_rs, 0)

    def left(n, carry):
        for part in range(2):
            sib_copy(n, part).wait_send()

        @pl.when(lax.rem(n, 4) != lax.rem(row, 4))
        def _():
            e_copy(n).wait_send()

        return carry

    lax.fori_loop(0, n_z, left, 0)

    def left_x(s, carry):
        x_copy(s).wait_send()
        bias_copy(s).wait_send()
        return carry

    lax.fori_loop(0, 4, left_x, 0)
    recv_all(g_wait, n_row)
    sent_all(g_copy, n_row)


def body(
    tokens, restype, type_table, key_mask, pair, w_bias, w_query, w_key, w_value, w_gate, cotangent
):
    n_row = lax.axis_size("row")
    n_col = lax.axis_size("col")
    n_z = n_col // 2
    samples = tokens.shape[0] * lax.axis_size("samp")
    total_tokens = tokens.shape[1] * n_col
    vmem = pl.BlockSpec(memory_space=pltpu.VMEM)
    hbm = pl.BlockSpec(memory_space=pl.ANY)
    dma = pltpu.SemaphoreType.DMA
    token_grad, weight_grad, pair_grad = pl.pallas_call(
        functools.partial(kernel, (n_row, n_col, total_tokens, samples)),
        out_shape=(
            pltpu.VMEM((4, 64, D), BF),
            pltpu.VMEM((H, C), F32),
            pltpu.VMEM((128, 64, C), BF),
        ),
        in_specs=[vmem] * 6 + [hbm] * 5,
        out_specs=(vmem, vmem, vmem),
        scratch_shapes=[
            pltpu.VMEM((D, D), BF),
            pltpu.VMEM((D, D), BF),
            pltpu.VMEM((D, D), BF),
            pltpu.VMEM((D, D), BF),
            pltpu.VMEM((128, 64, C), BF),
            pltpu.VMEM((8192, C), F32),
            pltpu.VMEM((64, 128, C), F32),
            pltpu.VMEM((64, 128, C), F32),
            pltpu.VMEM((H * 64, 128), F32),
            pltpu.VMEM((64, D), F32),
            pltpu.VMEM((4, 64, D), BF),
            pltpu.VMEM((4, 64, D), BF),
            pltpu.VMEM((32, D), F32),
            pltpu.VMEM((2, 32, D), BF),
            pltpu.VMEM((4, 2, 128, D), BF),
            pltpu.VMEM((256, GW), BF),
            pltpu.VMEM((64, 128), F32),
            pltpu.VMEM((16, 256, 128), F32),
            pltpu.VMEM((16, 256, 128), F32),
            pltpu.VMEM((4, D, 128), F32),
            pltpu.VMEM((16, 16, 128), F32),
            pltpu.VMEM((16, 16, 128), F32),
            pltpu.VMEM((16, 128), F32),
            pltpu.VMEM((16, 16, 128), F32),
            pltpu.VMEM((NG, 256, 128), F32),
            pltpu.VMEM((NG, 256, 128), F32),
            pltpu.VMEM((16, 256, 128), BF),
            pltpu.VMEM((16, 256, 128), BF),
            pltpu.VMEM((4, 64, D), F32),
            pltpu.VMEM((2, 4, 32, D), F32),
            pltpu.VMEM((2, 32, D), F32),
            pltpu.VMEM((4, 2, 128, D), F32),
            pltpu.VMEM((4, 2, 64, D), F32),
            pltpu.VMEM((4, 2, 64, D), F32),
            pltpu.VMEM((4, 4, 2, 16, D), F32),
            pltpu.VMEM((2, 32, D), F32),
            pltpu.VMEM((2, 32, D), F32),
            pltpu.VMEM((64, 16, 128), BF),
            pltpu.VMEM((n_col, H, C), F32),
            pltpu.VMEM((2, H, C), F32),
            pltpu.VMEM((n_row, H, C), F32),
            dma((4,)),
            dma,
            dma((3,)),
            dma((16,)),
            dma((16,)),
            dma((16,)),
            dma((16,)),
            dma((n_col,)),
            dma((n_col,)),
            dma((n_col,)),
            dma((n_col,)),
            dma((n_row,)),
            dma((n_row,)),
            dma((2,)),
            dma((4,)),
            dma((4,)),
            dma((16,)),
            dma((16,)),
            dma((NG,)),
            dma((NG,)),
            dma((3,)),
            dma((n_row,)),
            dma((n_row,)),
            dma((n_col,)),
            dma((n_col,)),
            dma((n_row,)),
            dma((n_row,)),
        ],
        compiler_params=pltpu.CompilerParams(
            collective_id=0, has_side_effects=True, vmem_limit_bytes=60 * 1024 * 1024
        ),
    )(
        tokens,
        restype.reshape(1, 64),
        type_table,
        key_mask.reshape(1, 64),
        w_bias.T,
        cotangent,
        w_query,
        w_key,
        w_value,
        w_gate,
        pair,
    )
    return (token_grad, pair_grad, weight_grad.T)


def solution(mesh):
    placed = (
        P("samp", "col", None),
        P("col"),
        P(),
        P("col"),
        P("row", "col", None),
        P(),
        P(),
        P(),
        P(),
        P(),
        P("samp", "col", None),
    )
    return jax.shard_map(
        body,
        mesh=mesh,
        in_specs=placed,
        out_specs=(P("samp", "col", None), P("row", "col", None), P()),
        check_vma=False,
    )
```

```python
import functools
import math

import jax
import jax.numpy as jnp
from jax import lax
from jax.experimental import pallas as pl
from jax.experimental.pallas import tpu as pltpu
from jax.sharding import PartitionSpec as P

D = 768
H = 16
CH = 48
C = 128
NTYPE = 32
GROUP = 4
NG = H // GROUP
GW = GROUP * CH
EPS = 1e-05
NEG = -1000000000.0
BF = jnp.bfloat16
F32 = jnp.float32
MESH = pl.DeviceIdType.MESH


def dot_nn(a, b):
    return jnp.dot(a, b, preferred_element_type=F32)


def dot_nt(a, b):
    return lax.dot_general(a, b, (((1,), (1,)), ((), ())), preferred_element_type=F32)


def dot_tn(a, b):
    return lax.dot_general(a, b, (((0,), (0,)), ((), ())), preferred_element_type=F32)


def split(x):
    high = x.astype(BF)
    return high, (x - high.astype(F32)).astype(BF)


def norm(x):
    centred = x - jnp.mean(x, axis=-1, keepdims=True)
    inv = lax.rsqrt(jnp.mean(centred * centred, axis=-1, keepdims=True) + EPS)
    return centred * inv, inv


def norm_back(grad, normed, inv):
    return inv * (
        grad
        - jnp.mean(grad, axis=-1, keepdims=True)
        - normed * jnp.mean(grad * normed, axis=-1, keepdims=True)
    )


def kernel(
    sizes,
    tok_ref,
    rest_ref,
    table_ref,
    mask_ref,
    wbt_ref,
    cot_ref,
    wq_hbm,
    wk_hbm,
    wv_hbm,
    wg_hbm,
    pair_hbm,
    tg_ref,
    bw_ref,
    pg_ref,
    wq_ref,
    wk_ref,
    wv_ref,
    wg_ref,
    pair_ref,
    raw_ref,
    nrm_ref,
    inv_ref,
    bias_ref,
    emb_ref,
    k_ref,
    v_ref,
    sig_ref,
    qgs_ref,
    qg_ref,
    bdm_ref,
    keep_ref,
    e_ref,
    dp_ref,
    ot_ref,
    st_ref,
    str_ref,
    res_ref,
    resr_ref,
    gbs_ref,
    gbr_ref,
    gr_ref,
    pr_ref,
    dkv_ref,
    ekv_ref,
    ey_ref,
    oa_ref,
    oas_ref,
    oa_ref2,
    or_ref,
    dq_ref,
    dqs_ref,
    dq_ref2,
    dqr_ref,
    pm_ref,
    pmr_ref,
    inner_ref,
    hr_ref,
    hs_ref,
    hr2_ref,
    w_sem,
    pair_sem,
    t_sem,
    ag_send,
    ag_recv,
    sib_send,
    sib_recv,
    b_send,
    b_recv,
    b2_send,
    b2_recv,
    e_send,
    e_recv,
    ey_sem,
    y_send,
    y_recv,
    x_send,
    x_recv,
    o_send,
    o_recv,
    d_send,
    d_recv,
    f_send,
    f_recv,
    pm_sem,
    g_send,
    g_recv,
    h_send,
    h_recv,
    h2_send,
    h2_recv,
):
    n_row, n_col, total_tokens, samples = sizes
    samp = lax.axis_index("samp")
    row = lax.axis_index("row")
    col = lax.axis_index("col")
    core = lax.rem(col, 2)
    z = col // 2
    n_z = n_col // 2
    scale = 1.0 / math.sqrt(CH)
    rest_row = row // 2
    own_tok = pl.multiple_of(lax.rem(row, 2) * 32, 32)

    def at_col(c):
        return (samp, row, c)

    def at_row(r):
        return (samp, r, col)

    sibling = at_col(z * 2 + 1 - core)

    def differ(a, b):
        return sum(lax.rem(a // bit + b // bit, 2) * bit for bit in (1, 2, 4))

    slice_here = differ(z, row)
    query_dev = (samp, z, slice_here * 2 + core)
    owner_dev = (samp, slice_here, row * 2 + core)
    is_self = row + z == 0
    other_samp = (1 - samp, row, col)

    def remote(src, dst, send, recv, device):
        return pltpu.make_async_remote_copy(
            src_ref=src,
            dst_ref=dst,
            send_sem=send,
            recv_sem=recv,
            device_id=device,
            device_id_type=MESH,
        )

    weights = [
        pltpu.make_async_copy(src, dst, w_sem.at[n])
        for n, (src, dst) in enumerate(
            ((wq_hbm, wq_ref), (wg_hbm, wg_ref), (wk_hbm, wk_ref), (wv_hbm, wv_ref))
        )
    ]
    for copy in weights:
        copy.start()
    pair_copy = pltpu.make_async_copy(pair_hbm, pair_ref, pair_sem)
    pair_copy.start()

    barrier = pltpu.get_barrier_semaphore()

    def greet(device):
        pl.semaphore_signal(barrier, inc=1, device_id=device, device_id_type=MESH)

    def greet_col(d, carry):
        greet(at_col(lax.rem(col + d, n_col)))
        return carry

    def greet_row(d, carry):
        greet(at_row(lax.rem(row + d, n_row)))
        return carry

    lax.fori_loop(1, n_col, greet_col, 0)
    lax.fori_loop(1, n_row, greet_row, 0)
    greet(other_samp)

    @pl.when(jnp.logical_not(is_self))
    def _():
        greet(query_dev)
        greet(owner_dev)

    onehot = jnp.where(rest_ref[...] == lax.broadcasted_iota(jnp.int32, (NTYPE, 64), 0), 1.0, 0.0)
    emb_ref[...] = dot_tn(onehot.astype(BF), table_ref[...])
    own_rows = pl.ds(own_tok, 32)
    own_normed, own_inv = norm(tok_ref[rest_row, own_rows, :].astype(F32) + emb_ref[own_rows, :])
    own_act = own_normed.astype(BF)
    def region(number, part):
        start = pl.multiple_of(core * 64 + lax.rem(number, 2) * 32, 32)
        return qg_ref.at[number // 2, part, pl.ds(start, 32), :]

    def to_query(part):
        mine = qgs_ref.at[part]
        return remote(mine, region(row, part), t_sem.at[part], t_sem.at[2 + part], query_dev)

    def to_self(part):
        return pltpu.make_async_copy(
            qgs_ref.at[part], region(slice_here, part), t_sem.at[4 + part]
        )

    def swap_start(part):
        @pl.when(jnp.logical_not(is_self))
        def _():
            to_query(part).start()

        @pl.when(is_self)
        def _():
            to_self(part).start()

    def swap_wait(part):
        @pl.when(jnp.logical_not(is_self))
        def _():
            theirs = region(slice_here, part)
            remote(
                qgs_ref.at[part], theirs, t_sem.at[part], t_sem.at[2 + part], owner_dev
            ).wait_recv()

        @pl.when(is_self)
        def _():
            to_self(part).wait()

    weights[0].wait()
    qgs_ref[0] = dot_nn(own_act, wq_ref[...]).astype(BF)

    @pl.when(is_self)
    def _():
        pl.semaphore_wait(barrier, n_col + n_row - 1)

    @pl.when(jnp.logical_not(is_self))
    def _():
        pl.semaphore_wait(barrier, n_col + n_row + 1)

    swap_start(0)
    weights[1].wait()
    gate = dot_nn(own_act, wg_ref[...]).astype(BF).astype(F32)
    sig = jax.nn.sigmoid(gate)
    sig_ref[...] = sig
    own_cot = cot_ref[rest_row, own_rows, :].astype(F32)
    qgs_ref[1] = (own_cot * sig).astype(BF)
    swap_start(1)

    weights[2].wait()
    weights[3].wait()

    def project(s, carry):
        normed, _ = norm(tok_ref[s].astype(F32) + emb_ref[...])
        act = normed.astype(BF)
        k_ref[s] = dot_nn(act, wk_ref[...]).astype(BF)
        v_ref[s] = dot_nn(act, wv_ref[...]).astype(BF)
        return carry

    lax.fori_loop(0, 4, project, 0)
    lane = lax.broadcasted_iota(jnp.int32, (64, GW), 1)
    for h in range(GROUP):
        inside = jnp.logical_and(lane >= h * CH, lane < (h + 1) * CH)
        bdm_ref[h * 64 : (h + 1) * 64, :] = jnp.where(inside, 1.0, 0.0).astype(BF)
    first_row = lax.broadcasted_iota(jnp.int32, (16, 64), 0) == 0
    kept = jnp.where(jnp.logical_and(mask_ref[...] == 1, first_row), 1.0, 0.0)
    keep_ref[...] = dot_tn(kept.astype(BF), jnp.ones((16, 128), BF))
    pair_copy.wait()

    def widen(n, carry):
        raw_ref[pl.ds(pl.multiple_of(n * 512, 512), 512), :] = (
            pair_ref[pl.ds(n * 8, 8)].astype(F32).reshape(512, C)
        )
        return carry

    lax.fori_loop(0, 16, widen, 0)
    def part_of(zz, kk, part):
        number = differ(zz, row)
        start = pl.multiple_of(kk * 64 + lax.rem(number, 2) * 32, 32)
        return qg_ref.at[number // 2, part, pl.ds(start, 32), :]

    def ag_copy(way, part, step):
        origin = lax.rem(z + n_z - way * step, n_z)
        mine = part_of(origin, core, part)
        sem = (part * 2 + (way + 1) // 2) * 4 + step
        there = at_col(lax.rem(z + n_z + way, n_z) * 2 + core)
        return remote(mine, mine, ag_send.at[sem], ag_recv.at[sem], there)

    def ag_wait(way, part, step):
        origin = lax.rem(z + 2 * n_z - way * (step + 1), n_z)
        mine = part_of(origin, core, part)
        sem = (part * 2 + (way + 1) // 2) * 4 + step
        return remote(mine, mine, ag_send.at[sem], ag_recv.at[sem], sibling)

    def sib_copy(zz, part):
        mine = part_of(zz, core, part)
        sem = zz * 2 + part
        return remote(mine, mine, sib_send.at[sem], sib_recv.at[sem], sibling)

    def sib_wait(zz, part):
        theirs = part_of(zz, 1 - core, part)
        sem = zz * 2 + part
        return remote(theirs, theirs, sib_send.at[sem], sib_recv.at[sem], sibling)

    def last_step(way, part):
        return 3 if (way == 1) == (part == 0) else 2

    wbt = wbt_ref[...]
    wbt_wide = jnp.concatenate([wbt, wbt], axis=1)
    mean_one = jnp.full((C, C), 1.0 / C, BF)
    mean_two = jnp.full((2 * C, C), 1.0 / C, BF)

    def pair_forward(n, carry):
        first = n * 4
        values = jnp.concatenate(
            [raw_ref[pl.ds(first + u, 128, stride=64), :] for u in range(4)], axis=0
        )
        centred = values - dot_nn(values.astype(BF), mean_one)
        variance = dot_nn(jnp.concatenate(split(centred * centred), axis=1), mean_two)
        inv = lax.rsqrt(variance + EPS)
        normed = centred * inv
        nrm_ref[pl.ds(first, 4)] = normed.reshape(4, 128, C)
        inv_ref[pl.ds(first, 4)] = inv.reshape(4, 128, C)
        both = jnp.concatenate(split(normed), axis=1)
        for u in range(4):
            bias_ref[pl.ds(first + u, H, stride=64), :] = dot_nt(
                wbt_wide, both[u * 128 : (u + 1) * 128]
            )
        return carry

    lax.fori_loop(0, 8, pair_forward, 0)
    for part in range(2):
        swap_wait(part)
        for way in (1, -1):
            ag_copy(way, part, 0).start()
        sib_copy(z, part).start()

    def gather_step(step, carry):
        for part in range(2):
            for way in (1, -1):

                @pl.when(step <= last_step(way, part))
                def _():
                    ag_wait(way, part, step).wait_recv()

                @pl.when(step < last_step(way, part))
                def _():
                    ag_copy(way, part, step + 1).start()

                @pl.when(step <= last_step(way, part))
                def _():
                    sib_copy(lax.rem(z + 2 * n_z - way * (step + 1), n_z), part).start()

        return carry

    def gather_and_pair(step, carry):
        for n in range(2):
            pair_forward(8 + step * 2 + n, 0)
        return gather_step(step, carry)

    lax.fori_loop(0, 4, gather_and_pair, 0)

    def sib_arrive(zz, carry):
        for part in range(2):
            sib_wait(zz, part).wait_recv()
        return carry

    lax.fori_loop(0, n_z, sib_arrive, 0)

    def blocks(ref, s, g):
        one = ref[s, :, g * GW : (g + 1) * GW]
        return jnp.concatenate([one] * GROUP, axis=0) * bdm_ref[...]

    def b_copy(c):
        return remote(st_ref.at[c], str_ref.at[col], b_send.at[c], b_recv.at[col], at_col(c))

    def b_wait(d):
        c = lax.rem(col + n_col - d, n_col)
        return remote(st_ref.at[c], str_ref.at[c], b_send.at[c], b_recv.at[c], at_col(c))

    def forward(s, carry):
        keep = jnp.broadcast_to(keep_ref[...][None], (GROUP, 64, 128)) > 0.5
        for g in range(NG):
            sg = s * NG + g
            key_b = blocks(k_ref, s, g)
            value_b = blocks(v_ref, s, g)
            query = qg_ref[s, 0, :, g * GW : (g + 1) * GW]
            gout = qg_ref[s, 1, :, g * GW : (g + 1) * GW]
            scores = dot_nt(key_b, query) * scale + bias_ref[g * 256 : (g + 1) * 256, :]
            scores = jnp.where(keep, scores.reshape(GROUP, 64, 128), NEG)
            top = jnp.max(scores, axis=1)
            expo = jnp.exp(scores - top[:, None, :])
            expo_b = expo.astype(BF)
            pre = dot_nt(value_b, gout).reshape(GROUP, 64, 128)
            st_ref[sg, 0:4, :] = top
            st_ref[sg, 4:8, :] = jnp.sum(expo, axis=1)
            st_ref[sg, 8:12, :] = jnp.sum(expo_b.astype(F32) * pre, axis=1)
            e_ref[sg] = expo.reshape(256, 128)
            dp_ref[sg] = pre.reshape(256, 128)

            @pl.when(sg != col)
            def _():
                b_copy(sg).start()

            ot_ref[s, g * GW : (g + 1) * GW, :] = dot_tn(value_b, expo_b.reshape(256, 128))
        return carry

    lax.fori_loop(0, 4, forward, 0)

    def b2_copy(d):
        c = lax.rem(col + d, n_col)
        return remote(res_ref, resr_ref.at[col], b2_send.at[d], b2_recv.at[col], at_col(c))

    def b2_wait(d):
        c = lax.rem(col + n_col - d, n_col)
        return remote(res_ref, resr_ref.at[c], b2_send.at[d], b2_recv.at[c], at_col(c))

    def start_all(make, count):
        def step(d, carry):
            make(d).start()
            return carry

        lax.fori_loop(1, count, step, 0)

    def recv_all(make, count):
        def step(d, carry):
            make(d).wait_recv()
            return carry

        lax.fori_loop(1, count, step, 0)

    def sent_all(make, count):
        def step(d, carry):
            make(d).wait_send()
            return carry

        lax.fori_loop(1, count, step, 0)

    str_ref[col] = st_ref[col]
    recv_all(b_wait, n_col)
    parts = str_ref[...]
    tops = parts[:, 0:4, :]
    top_all = jnp.max(tops, axis=0)
    weight = jnp.exp(tops - top_all[None])
    inv_total = 1.0 / jnp.sum(parts[:, 4:8, :] * weight, axis=0)
    delta = jnp.sum(parts[:, 8:12, :] * weight, axis=0) * inv_total
    res_ref[0:4, :] = top_all
    res_ref[4:8, :] = inv_total
    res_ref[8:12, :] = delta
    resr_ref[col] = res_ref[...]
    start_all(b2_copy, n_col)
    recv_all(b2_wait, n_col)

    def e_copy(r):
        start = pl.multiple_of(lax.rem(r, 2) * 32, 32)
        return remote(
            dkv_ref.at[r // 2, pl.ds(start, 32), :],
            ekv_ref.at[r // 4, lax.rem(row, 4)],
            e_send.at[r],
            e_recv.at[(r // 4) * 4 + lax.rem(row, 4)],
            at_row((row // 4) * 4 + lax.rem(r, 4)),
        )

    def e_wait(hi, d):
        x = lax.rem(row + 4 - d, 4)
        return remote(
            dkv_ref.at[0, pl.ds(0, 32), :],
            ekv_ref.at[hi, x],
            e_send.at[hi * 4 + x],
            e_recv.at[hi * 4 + x],
            at_row((row // 4) * 4 + x),
        )

    def e_sum(hi):
        for d in range(1, 4):
            e_wait(hi, d).wait_recv()
        r = hi * 4 + lax.rem(row, 4)
        start = pl.multiple_of(lax.rem(r, 2) * 32, 32)
        ekv_ref[hi, lax.rem(row, 4)] = dkv_ref[r // 2, pl.ds(start, 32), :]
        return jnp.sum(ekv_ref[hi], axis=0)

    my_half = pl.multiple_of(core * 64, 64)
    their_half = pl.multiple_of((1 - core) * 64, 64)

    def core_copy(src, dst, send, recv):
        def make(s):
            half = src.at[s, pl.ds(their_half, 64), :]
            return remote(half, dst.at[s], send.at[s], recv.at[s], sibling)

        return make

    y_copy = core_copy(oa_ref, oas_ref, y_send, y_recv)
    x_copy = core_copy(dq_ref, dqs_ref, x_send, x_recv)

    def first_left(way, part):
        return 4 if (way == 1) == (part == 0) else 3

    def ring(own, slots, send, recv):
        def own_part(zz, part):
            number = differ(zz, row)
            start = pl.multiple_of(lax.rem(number, 2) * 32 + part * 16, 16)
            return own.at[number // 2, pl.ds(start, 16), :]

        def slot(way, part, left):
            return slots.at[part * 2 + (way + 1) // 2, left - 1]

        def copy(way, part, left, src):
            sem = (part * 2 + (way + 1) // 2) * 4 + left - 1
            there = at_col(lax.rem(z + n_z + way, n_z) * 2 + core)
            return remote(src, slot(way, part, left), send.at[sem], recv.at[sem], there)

        def begin():
            for part in range(2):
                for way in (1, -1):
                    left = first_left(way, part)
                    target = lax.rem(z + n_z + way * left, n_z)
                    copy(way, part, left, own_part(target, part)).start()

        def step(t):
            for part in range(2):
                for way in (1, -1):
                    left = first_left(way, part) - t

                    @pl.when(left > 1)
                    def _():
                        here = slot(way, part, left)
                        copy(way, part, left, here).wait_recv()
                        target = lax.rem(z + 2 * n_z + way * (left - 1), n_z)
                        here[...] = here[...] + own_part(target, part)[...]
                        copy(way, part, left - 1, here).start()

        def finish(dst):
            for part in range(2):
                for way in (1, -1):
                    copy(way, part, 1, slot(way, part, 1)).wait_recv()
            for part in range(2):
                dst[part * 16 : (part + 1) * 16, :] = (
                    own_part(z, part)[...] + slot(1, part, 1)[...] + slot(-1, part, 1)[...]
                )

        def drain():
            for part in range(2):
                for way in (1, -1):

                    def sent(left, carry):
                        copy(way, part, left, slot(way, part, left)).wait_send()
                        return carry

                    lax.fori_loop(1, first_left(way, part) + 1, sent, 0)

        return begin, step, finish, drain

    o_begin, o_step, o_finish, o_drain = ring(oa_ref2, or_ref, o_send, o_recv)
    d_begin, d_step, d_finish, d_drain = ring(dq_ref2, dqr_ref, d_send, d_recv)

    def add_cores(copy, whole, other, out):
        def step(t, carry):
            s = lax.rem(t + rest_row, 4)
            copy(s).wait_recv()
            out[s] = whole[s, pl.ds(my_half, 64), :] + other[s]
            return carry

        lax.fori_loop(0, 4, step, 0)

    def hand_over(n):
        return remote(pm_ref.at[n], pmr_ref.at[n], pm_sem.at[n], pm_sem.at[2 + n], owner_dev)

    def hand_own(n):
        return pltpu.make_async_copy(pm_ref.at[n], pmr_ref.at[n], pm_sem.at[4 + n])

    def hand_start(n):
        @pl.when(jnp.logical_not(is_self))
        def _():
            hand_over(n).start()

        @pl.when(is_self)
        def _():
            hand_own(n).start()

    def hand_wait(n):
        @pl.when(jnp.logical_not(is_self))
        def _():
            hand_over(n).wait()

        @pl.when(is_self)
        def _():
            hand_own(n).wait()

    lane4 = lax.broadcasted_iota(jnp.int32, (64, GW), 1)

    def diagonal(full):
        picked = full[3 * 64 : 4 * 64]
        for h in (2, 1, 0):
            picked = jnp.where(lane4 < (h + 1) * CH, full[h * 64 : (h + 1) * 64], picked)
        return picked

    def factor_of(sg):
        return jnp.exp(st_ref[sg, 0:4, :] - resr_ref[sg, 0:4, :]) * resr_ref[sg, 4:8, :]

    def attended(t, carry):
        s = lax.rem(t + rest_row, 4)
        outs = []
        for g in range(NG):
            part = ot_ref[s, g * GW : (g + 1) * GW, :].reshape(GROUP, CH, 128)
            outs.append((part * factor_of(s * NG + g)[:, None, :]).reshape(GW, 128).T)
        oa_ref[s] = jnp.concatenate(outs, axis=1)
        y_copy(s).start()
        return carry

    lax.fori_loop(0, 4, attended, 0)

    def bias_copy(g):
        return remote(gbs_ref.at[g], gbr_ref.at[g], f_send.at[g], f_recv.at[g], other_samp)

    def score_grads(g, carry):
        total = jnp.zeros((256, 128), F32)
        for s in range(4):
            sg = s * NG + g
            factor = factor_of(sg)
            down = resr_ref[sg, 8:12, :]
            probs = e_ref[sg].reshape(GROUP, 64, 128) * factor[:, None, :]
            grads = probs * (dp_ref[sg].reshape(GROUP, 64, 128) - down[:, None, :])
            grads = grads.reshape(256, 128)
            total = total + grads
            gr_ref[sg] = grads.astype(BF)
            pr_ref[sg] = probs.reshape(256, 128).astype(BF)
        gbs_ref[g] = total
        bias_copy(g).start()
        return carry

    lax.fori_loop(0, NG, score_grads, 0)

    add_cores(y_copy, oa_ref, oas_ref, oa_ref2)
    o_begin()

    def query_side(t, carry):
        s = lax.rem(t + rest_row, 4)
        queries = []
        for g in range(NG):
            queries.append(dot_tn(gr_ref[s * NG + g], blocks(k_ref, s, g)) * scale)
        dq_ref[s] = jnp.concatenate(queries, axis=1)
        x_copy(s).start()
        return carry

    lax.fori_loop(0, 4, query_side, 0)
    add_cores(x_copy, dq_ref, dqs_ref, dq_ref2)
    d_begin()
    o_step(0)

    def back_project(grad, weight_ref):
        both = dot_nt(jnp.concatenate(split(grad), axis=0), weight_ref[...])
        half = grad.shape[0]
        return both[0:half] + both[half:]

    def backward(t, carry):
        s = lax.rem(t + rest_row, 4)
        keys, values = [], []
        for g in range(NG):
            sg = s * NG + g
            query = qg_ref[s, 0, :, g * GW : (g + 1) * GW]
            gout = qg_ref[s, 1, :, g * GW : (g + 1) * GW]
            keys.append(diagonal(dot_nn(gr_ref[sg], query)) * scale)
            values.append(diagonal(dot_nn(pr_ref[sg], gout)))
        dkv_ref[s] = back_project(jnp.concatenate(keys, axis=1), wk_ref) + back_project(
            jnp.concatenate(values, axis=1), wv_ref
        )
        for half in range(2):
            r = s * 2 + half

            @pl.when(lax.rem(r, 4) != lax.rem(row, 4))
            def _():
                e_copy(r).start()

        return carry

    def backward_and_pass(n, carry):
        lax.fori_loop(n * 2, n * 2 + 2, backward, 0)
        o_step(n + 1)
        d_step(n)
        return carry

    lax.fori_loop(0, 2, backward_and_pass, 0)

    def bias_arrive(g, carry):
        bias_copy(g).wait_recv()
        return carry

    lax.fori_loop(0, NG, bias_arrive, 0)
    summed = (gbs_ref[...] + gbr_ref[...]).reshape(H * 64, 128)
    inner = jnp.sum((summed * bias_ref[...]).reshape(H, 64, 128), axis=0) * (1.0 / C)
    bias_ref[...] = summed
    inner_h = inner.astype(BF).astype(F32)
    inner_l = inner - inner_h
    which = lax.broadcasted_iota(jnp.int32, (64, 16, 128), 1)
    inner_ref[...] = jnp.where(
        which == 0, inner_h[:, None, :], jnp.where(which == 1, inner_l[:, None, :], 0.0)
    ).astype(BF)
    weight = wbt.astype(F32) * (total_tokens / samples)
    weight_h, weight_l = split(weight - jnp.mean(weight, axis=1, keepdims=True))
    blank = jnp.zeros((H, C), BF)
    ones = jnp.full((H, C), total_tokens / samples, BF)
    spread_w = jnp.concatenate(
        [
            jnp.concatenate([weight_h, weight_h, weight_l, blank], axis=0),
            jnp.concatenate([blank, blank, blank, ones], axis=0),
        ],
        axis=1,
    )

    def pair_backward(n, acc):
        grads, normeds = [], []
        for u in range(4):
            j = n * 4 + u
            high, low = split(bias_ref[pl.ds(j, H, stride=64), :])
            both = jnp.concatenate([high, low], axis=0)
            normed = nrm_ref[j]
            wide = dot_tn(jnp.concatenate([both, high, inner_ref[j]], axis=0), spread_w)
            raw_ref[pl.ds(j, 128, stride=64), :] = inv_ref[j] * (
                wide[:, 0:C] - normed * wide[:, C:]
            )
            grads.append(both)
            normeds.append(jnp.concatenate(split(normed), axis=1))
        for u in (0, 2):
            acc = acc + dot_nn(
                jnp.concatenate(grads[u : u + 2], axis=1),
                jnp.concatenate(normeds[u : u + 2], axis=0),
            )
        return acc

    acc = lax.fori_loop(0, 8, pair_backward, jnp.zeros((2 * H, 2 * C), F32))
    d_step(2)
    o_finish(pm_ref.at[0])
    hand_start(0)

    ey_copy = remote(
        ey_ref.at[0], ey_ref.at[1], ey_sem.at[0], ey_sem.at[1], at_row(lax.rem(row + 4, n_row))
    )
    ey_ref[0] = e_sum(1 - row // 4)
    ey_copy.start()
    acc = lax.fori_loop(8, 16, pair_backward, acc)

    def weight_copy(d):
        c = lax.rem(col + d, n_col)
        return remote(hs_ref.at[0], hr_ref.at[col], h_send.at[d], h_recv.at[col], at_col(c))

    def weight_wait(d):
        c = lax.rem(col + n_col - d, n_col)
        return remote(hs_ref.at[0], hr_ref.at[c], h_send.at[d], h_recv.at[c], at_col(c))

    hs_ref[0] = (acc[0:H, 0:C] + acc[H:, 0:C]) + (acc[0:H, C:] + acc[H:, C:])
    start_all(weight_copy, n_col)
    hr_ref[col] = hs_ref[0]
    d_finish(pm_ref.at[1])
    hand_start(1)

    def narrow(n, carry):
        pg_ref[pl.ds(n * 8, 8)] = (
            raw_ref[pl.ds(pl.multiple_of(n * 512, 512), 512), :].reshape(8, 64, C).astype(BF)
        )
        return carry

    lax.fori_loop(0, 16, narrow, 0)

    recv_all(weight_wait, n_col)
    hs_ref[1] = jnp.sum(hr_ref[...], axis=0)

    def weight2_copy(d):
        r = lax.rem(row + d, n_row)
        return remote(hs_ref.at[1], hr2_ref.at[row], h2_send.at[d], h2_recv.at[row], at_row(r))

    def weight2_wait(d):
        r = lax.rem(row + n_row - d, n_row)
        return remote(hs_ref.at[1], hr2_ref.at[r], h2_send.at[d], h2_recv.at[r], at_row(r))

    start_all(weight2_copy, n_row)
    hr2_ref[row] = hs_ref[1]

    total = e_sum(row // 4)
    ey_copy.wait_recv()
    total = total + ey_ref[1]

    hand_wait(0)
    hand_wait(1)
    total = total + back_project(pmr_ref[1], wq_ref)
    own_sig = sig_ref[...]
    cot = cot_ref[rest_row, own_rows, :].astype(F32)
    grad_gate = (cot * pmr_ref[0] * own_sig * (1.0 - own_sig)).astype(BF)
    total = total + dot_nt(grad_gate, wg_ref[...])
    own_normed, own_inv = norm(tok_ref[rest_row, own_rows, :].astype(F32) + emb_ref[own_rows, :])
    tg_ref[rest_row, own_rows, :] = norm_back(total, own_normed, own_inv).astype(BF)

    def g_copy(d):
        r = lax.rem(row + d, n_row)
        mine = tg_ref.at[rest_row, own_rows, :]
        return remote(mine, mine, g_send.at[d], g_recv.at[row], at_row(r))

    def g_wait(d):
        r = lax.rem(row + n_row - d, n_row)
        start = pl.multiple_of(lax.rem(r, 2) * 32, 32)
        theirs = tg_ref.at[r // 2, pl.ds(start, 32), :]
        return remote(theirs, theirs, g_send.at[d], g_recv.at[r], at_row(r))

    start_all(g_copy, n_row)
    recv_all(weight2_wait, n_row)
    bw_ref[...] = jnp.sum(hr2_ref[...], axis=0) * (1.0 / samples)

    @pl.when(jnp.logical_not(is_self))
    def _():
        for part in range(2):
            to_query(part).wait_send()

    sent_all(b2_copy, n_col)
    sent_all(weight_copy, n_col)
    sent_all(weight2_copy, n_row)
    ey_copy.wait_send()
    o_drain()
    d_drain()
    for part in range(2):
        for way in (1, -1):

            def left_ag(step, carry):
                ag_copy(way, part, step).wait_send()
                return carry

            lax.fori_loop(0, last_step(way, part) + 1, left_ag, 0)

    def left(n, carry):
        for part in range(2):
            sib_copy(n, part).wait_send()

        @pl.when(lax.rem(n, 4) != lax.rem(row, 4))
        def _():
            e_copy(n).wait_send()

        return carry

    lax.fori_loop(0, n_z, left, 0)

    def left_b(c, carry):
        @pl.when(c != col)
        def _():
            b_copy(c).wait_send()

        return carry

    lax.fori_loop(0, n_col, left_b, 0)

    def left_x(s, carry):
        x_copy(s).wait_send()
        y_copy(s).wait_send()
        bias_copy(s).wait_send()
        return carry

    lax.fori_loop(0, 4, left_x, 0)
    recv_all(g_wait, n_row)
    sent_all(g_copy, n_row)


def body(
    tokens, restype, type_table, key_mask, pair, w_bias, w_query, w_key, w_value, w_gate, cotangent
):
    n_row = lax.axis_size("row")
    n_col = lax.axis_size("col")
    n_z = n_col // 2
    samples = tokens.shape[0] * lax.axis_size("samp")
    total_tokens = tokens.shape[1] * n_col
    vmem = pl.BlockSpec(memory_space=pltpu.VMEM)
    hbm = pl.BlockSpec(memory_space=pl.ANY)
    dma = pltpu.SemaphoreType.DMA
    token_grad, weight_grad, pair_grad = pl.pallas_call(
        functools.partial(kernel, (n_row, n_col, total_tokens, samples)),
        out_shape=(
            pltpu.VMEM((4, 64, D), BF),
            pltpu.VMEM((H, C), F32),
            pltpu.VMEM((128, 64, C), BF),
        ),
        in_specs=[vmem] * 6 + [hbm] * 5,
        out_specs=(vmem, vmem, vmem),
        scratch_shapes=[
            pltpu.VMEM((D, D), BF),
            pltpu.VMEM((D, D), BF),
            pltpu.VMEM((D, D), BF),
            pltpu.VMEM((D, D), BF),
            pltpu.VMEM((128, 64, C), BF),
            pltpu.VMEM((8192, C), F32),
            pltpu.VMEM((64, 128, C), F32),
            pltpu.VMEM((64, 128, C), F32),
            pltpu.VMEM((H * 64, 128), F32),
            pltpu.VMEM((64, D), F32),
            pltpu.VMEM((4, 64, D), BF),
            pltpu.VMEM((4, 64, D), BF),
            pltpu.VMEM((32, D), F32),
            pltpu.VMEM((2, 32, D), BF),
            pltpu.VMEM((4, 2, 128, D), BF),
            pltpu.VMEM((256, GW), BF),
            pltpu.VMEM((64, 128), F32),
            pltpu.VMEM((16, 256, 128), F32),
            pltpu.VMEM((16, 256, 128), F32),
            pltpu.VMEM((4, D, 128), F32),
            pltpu.VMEM((16, 12, 128), F32),
            pltpu.VMEM((16, 12, 128), F32),
            pltpu.VMEM((12, 128), F32),
            pltpu.VMEM((16, 12, 128), F32),
            pltpu.VMEM((NG, 256, 128), F32),
            pltpu.VMEM((NG, 256, 128), F32),
            pltpu.VMEM((16, 256, 128), BF),
            pltpu.VMEM((16, 256, 128), BF),
            pltpu.VMEM((4, 64, D), F32),
            pltpu.VMEM((2, 4, 32, D), F32),
            pltpu.VMEM((2, 32, D), F32),
            pltpu.VMEM((4, 128, D), F32),
            pltpu.VMEM((4, 64, D), F32),
            pltpu.VMEM((4, 64, D), F32),
            pltpu.VMEM((4, 4, 16, D), F32),
            pltpu.VMEM((4, 128, D), F32),
            pltpu.VMEM((4, 64, D), F32),
            pltpu.VMEM((4, 64, D), F32),
            pltpu.VMEM((4, 4, 16, D), F32),
            pltpu.VMEM((2, 32, D), F32),
            pltpu.VMEM((2, 32, D), F32),
            pltpu.VMEM((64, 16, 128), BF),
            pltpu.VMEM((n_col, H, C), F32),
            pltpu.VMEM((2, H, C), F32),
            pltpu.VMEM((n_row, H, C), F32),
            dma((4,)),
            dma,
            dma((6,)),
            dma((16,)),
            dma((16,)),
            dma((16,)),
            dma((16,)),
            dma((n_col,)),
            dma((n_col,)),
            dma((n_col,)),
            dma((n_col,)),
            dma((n_row,)),
            dma((n_row,)),
            dma((2,)),
            dma((4,)),
            dma((4,)),
            dma((4,)),
            dma((4,)),
            dma((16,)),
            dma((16,)),
            dma((16,)),
            dma((16,)),
            dma((NG,)),
            dma((NG,)),
            dma((6,)),
            dma((n_row,)),
            dma((n_row,)),
            dma((n_col,)),
            dma((n_col,)),
            dma((n_row,)),
            dma((n_row,)),
        ],
        compiler_params=pltpu.CompilerParams(
            collective_id=0, has_side_effects=True, vmem_limit_bytes=60 * 1024 * 1024
        ),
    )(
        tokens,
        restype.reshape(1, 64),
        type_table,
        key_mask.reshape(1, 64),
        w_bias.T,
        cotangent,
        w_query,
        w_key,
        w_value,
        w_gate,
        pair,
    )
    return (token_grad, pair_grad, weight_grad.T)


def solution(mesh):
    placed = (
        P("samp", "col", None),
        P("col"),
        P(),
        P("col"),
        P("row", "col", None),
        P(),
        P(),
        P(),
        P(),
        P(),
        P("samp", "col", None),
    )
    return jax.shard_map(
        body,
        mesh=mesh,
        in_specs=placed,
        out_specs=(P("samp", "col", None), P("row", "col", None), P()),
        check_vma=False,
    )
```

```python
import functools
import math

import jax
import jax.numpy as jnp
from jax import lax
from jax.experimental import pallas as pl
from jax.experimental.pallas import tpu as pltpu
from jax.sharding import PartitionSpec as P

D = 768
H = 16
CH = 48
C = 128
NTYPE = 32
GROUP = 4
NG = H // GROUP
GW = GROUP * CH
EPS = 1e-05
NEG = -1000000000.0
BF = jnp.bfloat16
F32 = jnp.float32
MESH = pl.DeviceIdType.MESH


def dot_nn(a, b):
    return jnp.dot(a, b, preferred_element_type=F32)


def dot_nt(a, b):
    return lax.dot_general(a, b, (((1,), (1,)), ((), ())), preferred_element_type=F32)


def dot_tn(a, b):
    return lax.dot_general(a, b, (((0,), (0,)), ((), ())), preferred_element_type=F32)


def split(x):
    high = x.astype(BF)
    return high, (x - high.astype(F32)).astype(BF)


def norm(x):
    centred = x - jnp.mean(x, axis=-1, keepdims=True)
    inv = lax.rsqrt(jnp.mean(centred * centred, axis=-1, keepdims=True) + EPS)
    return centred * inv, inv


def norm_back(grad, normed, inv):
    return inv * (
        grad
        - jnp.mean(grad, axis=-1, keepdims=True)
        - normed * jnp.mean(grad * normed, axis=-1, keepdims=True)
    )


def kernel(
    sizes,
    tok_ref,
    rest_ref,
    table_ref,
    mask_ref,
    wbt_ref,
    cot_ref,
    wq_hbm,
    wk_hbm,
    wv_hbm,
    wg_hbm,
    pair_hbm,
    tg_ref,
    bw_ref,
    pg_ref,
    wq_ref,
    wk_ref,
    wv_ref,
    wg_ref,
    pair_ref,
    raw_ref,
    nrm_ref,
    inv_ref,
    bias_ref,
    emb_ref,
    k_ref,
    v_ref,
    sig_ref,
    qgs_ref,
    qg_ref,
    bdm_ref,
    keep_ref,
    e_ref,
    dp_ref,
    ot_ref,
    st_ref,
    str_ref,
    res_ref,
    resr_ref,
    gbs_ref,
    gbr_ref,
    gr_ref,
    pr_ref,
    dkv_ref,
    ekv_ref,
    ey_ref,
    oa_ref,
    oas_ref,
    oa_ref2,
    or_ref,
    dq_ref,
    dqs_ref,
    dq_ref2,
    dqr_ref,
    pm_ref,
    pmr_ref,
    inner_ref,
    hr_ref,
    hs_ref,
    hr2_ref,
    w_sem,
    pair_sem,
    t_sem,
    ag_send,
    ag_recv,
    sib_send,
    sib_recv,
    b_send,
    b_recv,
    b2_send,
    b2_recv,
    e_send,
    e_recv,
    ey_sem,
    y_send,
    y_recv,
    x_send,
    x_recv,
    o_send,
    o_recv,
    d_send,
    d_recv,
    f_send,
    f_recv,
    pm_sem,
    g_send,
    g_recv,
    h_send,
    h_recv,
    h2_send,
    h2_recv,
):
    n_row, n_col, total_tokens, samples = sizes
    samp = lax.axis_index("samp")
    row = lax.axis_index("row")
    col = lax.axis_index("col")
    core = lax.rem(col, 2)
    z = col // 2
    n_z = n_col // 2
    scale = 1.0 / math.sqrt(CH)
    rest_row = row // 2
    own_tok = pl.multiple_of(lax.rem(row, 2) * 32, 32)

    def at_col(c):
        return (samp, row, c)

    def at_row(r):
        return (samp, r, col)

    sibling = at_col(z * 2 + 1 - core)

    def differ(a, b):
        return sum(lax.rem(a // bit + b // bit, 2) * bit for bit in (1, 2, 4))

    slice_here = differ(z, row)
    query_dev = (samp, z, slice_here * 2 + core)
    owner_dev = (samp, slice_here, row * 2 + core)
    is_self = row + z == 0
    other_samp = (1 - samp, row, col)

    def remote(src, dst, send, recv, device):
        return pltpu.make_async_remote_copy(
            src_ref=src,
            dst_ref=dst,
            send_sem=send,
            recv_sem=recv,
            device_id=device,
            device_id_type=MESH,
        )

    barrier = pltpu.get_barrier_semaphore()

    def greet(device):
        pl.semaphore_signal(barrier, inc=1, device_id=device, device_id_type=MESH)

    def greet_col(d, carry):
        greet(at_col(lax.rem(col + d, n_col)))
        return carry

    def greet_row(d, carry):
        greet(at_row(lax.rem(row + d, n_row)))
        return carry

    lax.fori_loop(1, n_col, greet_col, 0)
    lax.fori_loop(1, n_row, greet_row, 0)
    greet(other_samp)

    @pl.when(jnp.logical_not(is_self))
    def _():
        greet(query_dev)
        greet(owner_dev)

    weights = [
        pltpu.make_async_copy(src, dst, w_sem.at[n])
        for n, (src, dst) in enumerate(
            ((wq_hbm, wq_ref), (wg_hbm, wg_ref), (wk_hbm, wk_ref), (wv_hbm, wv_ref))
        )
    ]
    for copy in weights:
        copy.start()
    pair_copy = pltpu.make_async_copy(pair_hbm, pair_ref, pair_sem)
    pair_copy.start()

    onehot = jnp.where(rest_ref[...] == lax.broadcasted_iota(jnp.int32, (NTYPE, 64), 0), 1.0, 0.0)
    emb_ref[...] = dot_tn(onehot.astype(BF), table_ref[...])
    own_rows = pl.ds(own_tok, 32)
    own_normed, own_inv = norm(tok_ref[rest_row, own_rows, :].astype(F32) + emb_ref[own_rows, :])
    own_act = own_normed.astype(BF)
    def region(number, part):
        start = pl.multiple_of(core * 64 + lax.rem(number, 2) * 32, 32)
        return qg_ref.at[number // 2, part, pl.ds(start, 32), :]

    def to_query(part):
        mine = qgs_ref.at[part]
        return remote(mine, region(row, part), t_sem.at[part], t_sem.at[2 + part], query_dev)

    def to_self(part):
        return pltpu.make_async_copy(
            qgs_ref.at[part], region(slice_here, part), t_sem.at[4 + part]
        )

    def swap_start(part):
        @pl.when(jnp.logical_not(is_self))
        def _():
            to_query(part).start()

        @pl.when(is_self)
        def _():
            to_self(part).start()

    def swap_wait(part):
        @pl.when(jnp.logical_not(is_self))
        def _():
            theirs = region(slice_here, part)
            remote(
                qgs_ref.at[part], theirs, t_sem.at[part], t_sem.at[2 + part], owner_dev
            ).wait_recv()

        @pl.when(is_self)
        def _():
            to_self(part).wait()

    weights[0].wait()
    qgs_ref[0] = dot_nn(own_act, wq_ref[...]).astype(BF)

    @pl.when(is_self)
    def _():
        pl.semaphore_wait(barrier, n_col + n_row - 1)

    @pl.when(jnp.logical_not(is_self))
    def _():
        pl.semaphore_wait(barrier, n_col + n_row + 1)

    swap_start(0)
    weights[1].wait()
    gate = dot_nn(own_act, wg_ref[...]).astype(BF).astype(F32)
    sig = jax.nn.sigmoid(gate)
    sig_ref[...] = sig
    own_cot = cot_ref[rest_row, own_rows, :].astype(F32)
    qgs_ref[1] = (own_cot * sig).astype(BF)
    swap_start(1)

    weights[2].wait()
    weights[3].wait()

    def project(s, carry):
        normed, _ = norm(tok_ref[s].astype(F32) + emb_ref[...])
        act = normed.astype(BF)
        k_ref[s] = dot_nn(act, wk_ref[...]).astype(BF)
        v_ref[s] = dot_nn(act, wv_ref[...]).astype(BF)
        return carry

    lax.fori_loop(0, 4, project, 0)
    lane = lax.broadcasted_iota(jnp.int32, (64, GW), 1)
    for h in range(GROUP):
        inside = jnp.logical_and(lane >= h * CH, lane < (h + 1) * CH)
        bdm_ref[h * 64 : (h + 1) * 64, :] = jnp.where(inside, 1.0, 0.0).astype(BF)
    first_row = lax.broadcasted_iota(jnp.int32, (16, 64), 0) == 0
    kept = jnp.where(jnp.logical_and(mask_ref[...] == 1, first_row), 1.0, 0.0)
    keep_ref[...] = dot_tn(kept.astype(BF), jnp.ones((16, 128), BF))
    pair_copy.wait()

    def widen(n, carry):
        raw_ref[pl.ds(pl.multiple_of(n * 512, 512), 512), :] = (
            pair_ref[pl.ds(n * 8, 8)].astype(F32).reshape(512, C)
        )
        return carry

    lax.fori_loop(0, 16, widen, 0)
    def part_of(zz, kk, part):
        number = differ(zz, row)
        start = pl.multiple_of(kk * 64 + lax.rem(number, 2) * 32, 32)
        return qg_ref.at[number // 2, part, pl.ds(start, 32), :]

    def ag_copy(way, part, step):
        origin = lax.rem(z + n_z - way * step, n_z)
        mine = part_of(origin, core, part)
        sem = (part * 2 + (way + 1) // 2) * 4 + step
        there = at_col(lax.rem(z + n_z + way, n_z) * 2 + core)
        return remote(mine, mine, ag_send.at[sem], ag_recv.at[sem], there)

    def ag_wait(way, part, step):
        origin = lax.rem(z + 2 * n_z - way * (step + 1), n_z)
        mine = part_of(origin, core, part)
        sem = (part * 2 + (way + 1) // 2) * 4 + step
        return remote(mine, mine, ag_send.at[sem], ag_recv.at[sem], sibling)

    def sib_copy(zz, part):
        mine = part_of(zz, core, part)
        sem = zz * 2 + part
        return remote(mine, mine, sib_send.at[sem], sib_recv.at[sem], sibling)

    def sib_wait(zz, part):
        theirs = part_of(zz, 1 - core, part)
        sem = zz * 2 + part
        return remote(theirs, theirs, sib_send.at[sem], sib_recv.at[sem], sibling)

    def last_step(way, part):
        return 3 if (way == 1) == (part == 0) else 2

    wbt = wbt_ref[...]
    wbt_wide = jnp.concatenate([wbt, wbt], axis=1)
    mean_one = jnp.full((C, C), 1.0 / C, BF)
    mean_two = jnp.full((2 * C, C), 1.0 / C, BF)

    def pair_forward(n, carry):
        first = n * 4
        values = jnp.concatenate(
            [raw_ref[pl.ds(first + u, 128, stride=64), :] for u in range(4)], axis=0
        )
        centred = values - dot_nn(values.astype(BF), mean_one)
        variance = dot_nn(jnp.concatenate(split(centred * centred), axis=1), mean_two)
        inv = lax.rsqrt(variance + EPS)
        normed = centred * inv
        nrm_ref[pl.ds(first, 4)] = normed.reshape(4, 128, C)
        inv_ref[pl.ds(first, 4)] = inv.reshape(4, 128, C)
        both = jnp.concatenate(split(normed), axis=1)
        for u in range(4):
            bias_ref[pl.ds(first + u, H, stride=64), :] = dot_nt(
                wbt_wide, both[u * 128 : (u + 1) * 128]
            )
        return carry

    lax.fori_loop(0, 8, pair_forward, 0)
    for part in range(2):
        swap_wait(part)
        for way in (1, -1):
            ag_copy(way, part, 0).start()
        sib_copy(z, part).start()

    def gather_step(step, carry):
        for part in range(2):
            for way in (1, -1):

                @pl.when(step <= last_step(way, part))
                def _():
                    ag_wait(way, part, step).wait_recv()

                @pl.when(step < last_step(way, part))
                def _():
                    ag_copy(way, part, step + 1).start()

                @pl.when(step <= last_step(way, part))
                def _():
                    sib_copy(lax.rem(z + 2 * n_z - way * (step + 1), n_z), part).start()

        return carry

    def gather_and_pair(step, carry):
        for n in range(2):
            pair_forward(8 + step * 2 + n, 0)
        return gather_step(step, carry)

    lax.fori_loop(0, 4, gather_and_pair, 0)

    def sib_arrive(zz, carry):
        for part in range(2):
            sib_wait(zz, part).wait_recv()
        return carry

    lax.fori_loop(0, n_z, sib_arrive, 0)

    def blocks(ref, s, g):
        one = ref[s, :, g * GW : (g + 1) * GW]
        return jnp.concatenate([one] * GROUP, axis=0) * bdm_ref[...]

    def b_copy(c):
        return remote(st_ref.at[c], str_ref.at[col], b_send.at[c], b_recv.at[col], at_col(c))

    def b_wait(d):
        c = lax.rem(col + n_col - d, n_col)
        return remote(st_ref.at[c], str_ref.at[c], b_send.at[c], b_recv.at[c], at_col(c))

    def forward(s, carry):
        keep = jnp.broadcast_to(keep_ref[...][None], (GROUP, 64, 128)) > 0.5
        for g in range(NG):
            sg = s * NG + g
            key_b = blocks(k_ref, s, g)
            value_b = blocks(v_ref, s, g)
            query = qg_ref[s, 0, :, g * GW : (g + 1) * GW]
            gout = qg_ref[s, 1, :, g * GW : (g + 1) * GW]
            scores = dot_nt(key_b, query) * scale + bias_ref[g * 256 : (g + 1) * 256, :]
            scores = jnp.where(keep, scores.reshape(GROUP, 64, 128), NEG)
            top = jnp.max(scores, axis=1)
            expo = jnp.exp(scores - top[:, None, :])
            expo_b = expo.astype(BF)
            pre = dot_nt(value_b, gout).reshape(GROUP, 64, 128)
            st_ref[sg, 0:4, :] = top
            st_ref[sg, 4:8, :] = jnp.sum(expo, axis=1)
            st_ref[sg, 8:12, :] = jnp.sum(expo_b.astype(F32) * pre, axis=1)
            e_ref[sg] = expo.reshape(256, 128)
            dp_ref[sg] = pre.reshape(256, 128)

            @pl.when(sg != col)
            def _():
                b_copy(sg).start()

        return carry

    def partial_out(s, carry):
        for g in range(NG):
            expo_b = e_ref[s * NG + g].astype(BF)
            ot_ref[s, g * GW : (g + 1) * GW, :] = dot_tn(blocks(v_ref, s, g), expo_b)
        return carry

    lax.fori_loop(0, 4, forward, 0)

    def b2_copy(d):
        c = lax.rem(col + d, n_col)
        return remote(res_ref, resr_ref.at[col], b2_send.at[d], b2_recv.at[col], at_col(c))

    def b2_wait(d):
        c = lax.rem(col + n_col - d, n_col)
        return remote(res_ref, resr_ref.at[c], b2_send.at[d], b2_recv.at[c], at_col(c))

    def start_all(make, count):
        def step(d, carry):
            make(d).start()
            return carry

        lax.fori_loop(1, count, step, 0)

    def recv_all(make, count):
        def step(d, carry):
            make(d).wait_recv()
            return carry

        lax.fori_loop(1, count, step, 0)

    def sent_all(make, count):
        def step(d, carry):
            make(d).wait_send()
            return carry

        lax.fori_loop(1, count, step, 0)

    str_ref[col] = st_ref[col]
    lax.fori_loop(0, 4, partial_out, 0)
    recv_all(b_wait, n_col)
    parts = str_ref[...]
    tops = parts[:, 0:4, :]
    top_all = jnp.max(tops, axis=0)
    weight = jnp.exp(tops - top_all[None])
    inv_total = 1.0 / jnp.sum(parts[:, 4:8, :] * weight, axis=0)
    delta = jnp.sum(parts[:, 8:12, :] * weight, axis=0) * inv_total
    res_ref[0:4, :] = top_all
    res_ref[4:8, :] = inv_total
    res_ref[8:12, :] = delta
    resr_ref[col] = res_ref[...]
    start_all(b2_copy, n_col)
    recv_all(b2_wait, n_col)

    def e_copy(r):
        start = pl.multiple_of(lax.rem(r, 2) * 32, 32)
        return remote(
            dkv_ref.at[r // 2, pl.ds(start, 32), :],
            ekv_ref.at[r // 4, lax.rem(row, 4)],
            e_send.at[r],
            e_recv.at[(r // 4) * 4 + lax.rem(row, 4)],
            at_row((row // 4) * 4 + lax.rem(r, 4)),
        )

    def e_wait(hi, d):
        x = lax.rem(row + 4 - d, 4)
        return remote(
            dkv_ref.at[0, pl.ds(0, 32), :],
            ekv_ref.at[hi, x],
            e_send.at[hi * 4 + x],
            e_recv.at[hi * 4 + x],
            at_row((row // 4) * 4 + x),
        )

    def e_sum(hi):
        for d in range(1, 4):
            e_wait(hi, d).wait_recv()
        r = hi * 4 + lax.rem(row, 4)
        start = pl.multiple_of(lax.rem(r, 2) * 32, 32)
        ekv_ref[hi, lax.rem(row, 4)] = dkv_ref[r // 2, pl.ds(start, 32), :]
        return jnp.sum(ekv_ref[hi], axis=0)

    my_half = pl.multiple_of(core * 64, 64)
    their_half = pl.multiple_of((1 - core) * 64, 64)

    def core_copy(src, dst, send, recv):
        def make(s):
            half = src.at[s, pl.ds(their_half, 64), :]
            return remote(half, dst.at[s], send.at[s], recv.at[s], sibling)

        return make

    y_copy = core_copy(oa_ref, oas_ref, y_send, y_recv)
    x_copy = core_copy(dq_ref, dqs_ref, x_send, x_recv)

    def first_left(way, part):
        return 4 if (way == 1) == (part == 0) else 3

    def ring(own, slots, send, recv):
        def own_part(zz, part):
            number = differ(zz, row)
            start = pl.multiple_of(lax.rem(number, 2) * 32 + part * 16, 16)
            return own.at[number // 2, pl.ds(start, 16), :]

        def slot(way, part, left):
            return slots.at[part * 2 + (way + 1) // 2, left - 1]

        def copy(way, part, left, src):
            sem = (part * 2 + (way + 1) // 2) * 4 + left - 1
            there = at_col(lax.rem(z + n_z + way, n_z) * 2 + core)
            return remote(src, slot(way, part, left), send.at[sem], recv.at[sem], there)

        def begin():
            for part in range(2):
                for way in (1, -1):
                    left = first_left(way, part)
                    target = lax.rem(z + n_z + way * left, n_z)
                    copy(way, part, left, own_part(target, part)).start()

        def step(t):
            for part in range(2):
                for way in (1, -1):
                    left = first_left(way, part) - t

                    @pl.when(left > 1)
                    def _():
                        here = slot(way, part, left)
                        copy(way, part, left, here).wait_recv()
                        target = lax.rem(z + 2 * n_z + way * (left - 1), n_z)
                        here[...] = here[...] + own_part(target, part)[...]
                        copy(way, part, left - 1, here).start()

        def finish(dst):
            for part in range(2):
                for way in (1, -1):
                    copy(way, part, 1, slot(way, part, 1)).wait_recv()
            for part in range(2):
                dst[part * 16 : (part + 1) * 16, :] = (
                    own_part(z, part)[...] + slot(1, part, 1)[...] + slot(-1, part, 1)[...]
                )

        def drain():
            for part in range(2):
                for way in (1, -1):

                    def sent(left, carry):
                        copy(way, part, left, slot(way, part, left)).wait_send()
                        return carry

                    lax.fori_loop(1, first_left(way, part) + 1, sent, 0)

        return begin, step, finish, drain

    o_begin, o_step, o_finish, o_drain = ring(oa_ref2, or_ref, o_send, o_recv)
    d_begin, d_step, d_finish, d_drain = ring(dq_ref2, dqr_ref, d_send, d_recv)

    def add_cores(copy, whole, other, out):
        def step(t, carry):
            s = lax.rem(t + rest_row, 4)
            copy(s).wait_recv()
            out[s] = whole[s, pl.ds(my_half, 64), :] + other[s]
            return carry

        lax.fori_loop(0, 4, step, 0)

    def hand_over(n):
        return remote(pm_ref.at[n], pmr_ref.at[n], pm_sem.at[n], pm_sem.at[2 + n], owner_dev)

    def hand_own(n):
        return pltpu.make_async_copy(pm_ref.at[n], pmr_ref.at[n], pm_sem.at[4 + n])

    def hand_start(n):
        @pl.when(jnp.logical_not(is_self))
        def _():
            hand_over(n).start()

        @pl.when(is_self)
        def _():
            hand_own(n).start()

    def hand_wait(n):
        @pl.when(jnp.logical_not(is_self))
        def _():
            hand_over(n).wait()

        @pl.when(is_self)
        def _():
            hand_own(n).wait()

    lane4 = lax.broadcasted_iota(jnp.int32, (64, GW), 1)

    def diagonal(full):
        picked = full[3 * 64 : 4 * 64]
        for h in (2, 1, 0):
            picked = jnp.where(lane4 < (h + 1) * CH, full[h * 64 : (h + 1) * 64], picked)
        return picked

    def factor_of(sg):
        return jnp.exp(st_ref[sg, 0:4, :] - resr_ref[sg, 0:4, :]) * resr_ref[sg, 4:8, :]

    def attended(t, carry):
        s = lax.rem(t + rest_row, 4)
        outs = []
        for g in range(NG):
            part = ot_ref[s, g * GW : (g + 1) * GW, :].reshape(GROUP, CH, 128)
            outs.append((part * factor_of(s * NG + g)[:, None, :]).reshape(GW, 128).T)
        oa_ref[s] = jnp.concatenate(outs, axis=1)
        y_copy(s).start()
        return carry

    lax.fori_loop(0, 4, attended, 0)

    def bias_copy(g):
        return remote(gbs_ref.at[g], gbr_ref.at[g], f_send.at[g], f_recv.at[g], other_samp)

    def score_grads(g, carry):
        total = jnp.zeros((256, 128), F32)
        for s in range(4):
            sg = s * NG + g
            factor = factor_of(sg)
            down = resr_ref[sg, 8:12, :]
            probs = e_ref[sg].reshape(GROUP, 64, 128) * factor[:, None, :]
            grads = probs * (dp_ref[sg].reshape(GROUP, 64, 128) - down[:, None, :])
            grads = grads.reshape(256, 128)
            total = total + grads
            gr_ref[sg] = grads.astype(BF)
            pr_ref[sg] = probs.reshape(256, 128).astype(BF)
        gbs_ref[g] = total
        bias_copy(g).start()
        return carry

    lax.fori_loop(0, NG, score_grads, 0)

    add_cores(y_copy, oa_ref, oas_ref, oa_ref2)
    o_begin()

    def query_side(t, carry):
        s = lax.rem(t + rest_row, 4)
        queries = []
        for g in range(NG):
            queries.append(dot_tn(gr_ref[s * NG + g], blocks(k_ref, s, g)) * scale)
        dq_ref[s] = jnp.concatenate(queries, axis=1)
        x_copy(s).start()
        return carry

    lax.fori_loop(0, 4, query_side, 0)
    add_cores(x_copy, dq_ref, dqs_ref, dq_ref2)
    d_begin()
    o_step(0)

    def back_project(grad, weight_ref):
        both = dot_nt(jnp.concatenate(split(grad), axis=0), weight_ref[...])
        half = grad.shape[0]
        return both[0:half] + both[half:]

    def backward(t, carry):
        s = lax.rem(t + rest_row, 4)
        keys, values = [], []
        for g in range(NG):
            sg = s * NG + g
            query = qg_ref[s, 0, :, g * GW : (g + 1) * GW]
            gout = qg_ref[s, 1, :, g * GW : (g + 1) * GW]
            keys.append(diagonal(dot_nn(gr_ref[sg], query)) * scale)
            values.append(diagonal(dot_nn(pr_ref[sg], gout)))
        dkv_ref[s] = back_project(jnp.concatenate(keys, axis=1), wk_ref) + back_project(
            jnp.concatenate(values, axis=1), wv_ref
        )
        for half in range(2):
            r = s * 2 + half

            @pl.when(lax.rem(r, 4) != lax.rem(row, 4))
            def _():
                e_copy(r).start()

        return carry

    def backward_and_pass(n, carry):
        lax.fori_loop(n * 2, n * 2 + 2, backward, 0)
        o_step(n + 1)
        d_step(n)
        return carry

    lax.fori_loop(0, 2, backward_and_pass, 0)

    def bias_arrive(g, carry):
        bias_copy(g).wait_recv()
        return carry

    lax.fori_loop(0, NG, bias_arrive, 0)
    summed = (gbs_ref[...] + gbr_ref[...]).reshape(H * 64, 128)
    inner = jnp.sum((summed * bias_ref[...]).reshape(H, 64, 128), axis=0) * (1.0 / C)
    bias_ref[...] = summed
    inner_h = inner.astype(BF).astype(F32)
    inner_l = inner - inner_h
    which = lax.broadcasted_iota(jnp.int32, (64, 16, 128), 1)
    inner_ref[...] = jnp.where(
        which == 0, inner_h[:, None, :], jnp.where(which == 1, inner_l[:, None, :], 0.0)
    ).astype(BF)
    weight = wbt.astype(F32) * (total_tokens / samples)
    weight_h, weight_l = split(weight - jnp.mean(weight, axis=1, keepdims=True))
    blank = jnp.zeros((H, C), BF)
    ones = jnp.full((H, C), total_tokens / samples, BF)
    spread_w = jnp.concatenate(
        [
            jnp.concatenate([weight_h, weight_h, weight_l, blank], axis=0),
            jnp.concatenate([blank, blank, blank, ones], axis=0),
        ],
        axis=1,
    )

    def pair_backward(n, acc):
        grads, normeds = [], []
        for u in range(4):
            j = n * 4 + u
            high, low = split(bias_ref[pl.ds(j, H, stride=64), :])
            both = jnp.concatenate([high, low], axis=0)
            normed = nrm_ref[j]
            wide = dot_tn(jnp.concatenate([both, high, inner_ref[j]], axis=0), spread_w)
            raw_ref[pl.ds(j, 128, stride=64), :] = inv_ref[j] * (
                wide[:, 0:C] - normed * wide[:, C:]
            )
            grads.append(both)
            normeds.append(jnp.concatenate(split(normed), axis=1))
        for u in (0, 2):
            acc = acc + dot_nn(
                jnp.concatenate(grads[u : u + 2], axis=1),
                jnp.concatenate(normeds[u : u + 2], axis=0),
            )
        return acc

    acc = lax.fori_loop(0, 8, pair_backward, jnp.zeros((2 * H, 2 * C), F32))
    d_step(2)
    o_finish(pm_ref.at[0])
    hand_start(0)

    ey_copy = remote(
        ey_ref.at[0], ey_ref.at[1], ey_sem.at[0], ey_sem.at[1], at_row(lax.rem(row + 4, n_row))
    )
    ey_ref[0] = e_sum(1 - row // 4)
    ey_copy.start()
    acc = lax.fori_loop(8, 16, pair_backward, acc)

    def weight_copy(d):
        c = lax.rem(col + d, n_col)
        return remote(hs_ref.at[0], hr_ref.at[col], h_send.at[d], h_recv.at[col], at_col(c))

    def weight_wait(d):
        c = lax.rem(col + n_col - d, n_col)
        return remote(hs_ref.at[0], hr_ref.at[c], h_send.at[d], h_recv.at[c], at_col(c))

    hs_ref[0] = (acc[0:H, 0:C] + acc[H:, 0:C]) + (acc[0:H, C:] + acc[H:, C:])
    start_all(weight_copy, n_col)
    hr_ref[col] = hs_ref[0]
    d_finish(pm_ref.at[1])
    hand_start(1)

    def narrow(n, carry):
        pg_ref[pl.ds(n * 8, 8)] = (
            raw_ref[pl.ds(pl.multiple_of(n * 512, 512), 512), :].reshape(8, 64, C).astype(BF)
        )
        return carry

    lax.fori_loop(0, 16, narrow, 0)

    recv_all(weight_wait, n_col)
    hs_ref[1] = jnp.sum(hr_ref[...], axis=0)

    def weight2_copy(d):
        r = lax.rem(row + d, n_row)
        return remote(hs_ref.at[1], hr2_ref.at[row], h2_send.at[d], h2_recv.at[row], at_row(r))

    def weight2_wait(d):
        r = lax.rem(row + n_row - d, n_row)
        return remote(hs_ref.at[1], hr2_ref.at[r], h2_send.at[d], h2_recv.at[r], at_row(r))

    start_all(weight2_copy, n_row)
    hr2_ref[row] = hs_ref[1]

    total = e_sum(row // 4)
    ey_copy.wait_recv()
    total = total + ey_ref[1]

    own_normed, own_inv = norm(tok_ref[rest_row, own_rows, :].astype(F32) + emb_ref[own_rows, :])
    own_sig = sig_ref[...]
    cot = cot_ref[rest_row, own_rows, :].astype(F32)
    hand_wait(0)
    grad_gate = (cot * pmr_ref[0] * own_sig * (1.0 - own_sig)).astype(BF)
    total = total + dot_nt(grad_gate, wg_ref[...])
    hand_wait(1)
    total = total + back_project(pmr_ref[1], wq_ref)
    tg_ref[rest_row, own_rows, :] = norm_back(total, own_normed, own_inv).astype(BF)

    def g_copy(d):
        r = lax.rem(row + d, n_row)
        mine = tg_ref.at[rest_row, own_rows, :]
        return remote(mine, mine, g_send.at[d], g_recv.at[row], at_row(r))

    def g_wait(d):
        r = lax.rem(row + n_row - d, n_row)
        start = pl.multiple_of(lax.rem(r, 2) * 32, 32)
        theirs = tg_ref.at[r // 2, pl.ds(start, 32), :]
        return remote(theirs, theirs, g_send.at[d], g_recv.at[r], at_row(r))

    start_all(g_copy, n_row)
    recv_all(weight2_wait, n_row)
    bw_ref[...] = jnp.sum(hr2_ref[...], axis=0) * (1.0 / samples)

    @pl.when(jnp.logical_not(is_self))
    def _():
        for part in range(2):
            to_query(part).wait_send()

    sent_all(b2_copy, n_col)
    sent_all(weight_copy, n_col)
    sent_all(weight2_copy, n_row)
    ey_copy.wait_send()
    o_drain()
    d_drain()
    for part in range(2):
        for way in (1, -1):

            def left_ag(step, carry):
                ag_copy(way, part, step).wait_send()
                return carry

            lax.fori_loop(0, last_step(way, part) + 1, left_ag, 0)

    def left(n, carry):
        for part in range(2):
            sib_copy(n, part).wait_send()

        @pl.when(lax.rem(n, 4) != lax.rem(row, 4))
        def _():
            e_copy(n).wait_send()

        return carry

    lax.fori_loop(0, n_z, left, 0)

    def left_b(c, carry):
        @pl.when(c != col)
        def _():
            b_copy(c).wait_send()

        return carry

    lax.fori_loop(0, n_col, left_b, 0)

    def left_x(s, carry):
        x_copy(s).wait_send()
        y_copy(s).wait_send()
        bias_copy(s).wait_send()
        return carry

    lax.fori_loop(0, 4, left_x, 0)
    recv_all(g_wait, n_row)
    sent_all(g_copy, n_row)


def body(
    tokens, restype, type_table, key_mask, pair, w_bias, w_query, w_key, w_value, w_gate, cotangent
):
    n_row = lax.axis_size("row")
    n_col = lax.axis_size("col")
    n_z = n_col // 2
    samples = tokens.shape[0] * lax.axis_size("samp")
    total_tokens = tokens.shape[1] * n_col
    vmem = pl.BlockSpec(memory_space=pltpu.VMEM)
    hbm = pl.BlockSpec(memory_space=pl.ANY)
    dma = pltpu.SemaphoreType.DMA
    token_grad, weight_grad, pair_grad = pl.pallas_call(
        functools.partial(kernel, (n_row, n_col, total_tokens, samples)),
        out_shape=(
            pltpu.VMEM((4, 64, D), BF),
            pltpu.VMEM((H, C), F32),
            pltpu.VMEM((128, 64, C), BF),
        ),
        in_specs=[vmem] * 6 + [hbm] * 5,
        out_specs=(vmem, vmem, vmem),
        scratch_shapes=[
            pltpu.VMEM((D, D), BF),
            pltpu.VMEM((D, D), BF),
            pltpu.VMEM((D, D), BF),
            pltpu.VMEM((D, D), BF),
            pltpu.VMEM((128, 64, C), BF),
            pltpu.VMEM((8192, C), F32),
            pltpu.VMEM((64, 128, C), F32),
            pltpu.VMEM((64, 128, C), F32),
            pltpu.VMEM((H * 64, 128), F32),
            pltpu.VMEM((64, D), F32),
            pltpu.VMEM((4, 64, D), BF),
            pltpu.VMEM((4, 64, D), BF),
            pltpu.VMEM((32, D), F32),
            pltpu.VMEM((2, 32, D), BF),
            pltpu.VMEM((4, 2, 128, D), BF),
            pltpu.VMEM((256, GW), BF),
            pltpu.VMEM((64, 128), F32),
            pltpu.VMEM((16, 256, 128), F32),
            pltpu.VMEM((16, 256, 128), F32),
            pltpu.VMEM((4, D, 128), F32),
            pltpu.VMEM((16, 12, 128), F32),
            pltpu.VMEM((16, 12, 128), F32),
            pltpu.VMEM((12, 128), F32),
            pltpu.VMEM((16, 12, 128), F32),
            pltpu.VMEM((NG, 256, 128), F32),
            pltpu.VMEM((NG, 256, 128), F32),
            pltpu.VMEM((16, 256, 128), BF),
            pltpu.VMEM((16, 256, 128), BF),
            pltpu.VMEM((4, 64, D), F32),
            pltpu.VMEM((2, 4, 32, D), F32),
            pltpu.VMEM((2, 32, D), F32),
            pltpu.VMEM((4, 128, D), F32),
            pltpu.VMEM((4, 64, D), F32),
            pltpu.VMEM((4, 64, D), F32),
            pltpu.VMEM((4, 4, 16, D), F32),
            pltpu.VMEM((4, 128, D), F32),
            pltpu.VMEM((4, 64, D), F32),
            pltpu.VMEM((4, 64, D), F32),
            pltpu.VMEM((4, 4, 16, D), F32),
            pltpu.VMEM((2, 32, D), F32),
            pltpu.VMEM((2, 32, D), F32),
            pltpu.VMEM((64, 16, 128), BF),
            pltpu.VMEM((n_col, H, C), F32),
            pltpu.VMEM((2, H, C), F32),
            pltpu.VMEM((n_row, H, C), F32),
            dma((4,)),
            dma,
            dma((6,)),
            dma((16,)),
            dma((16,)),
            dma((16,)),
            dma((16,)),
            dma((n_col,)),
            dma((n_col,)),
            dma((n_col,)),
            dma((n_col,)),
            dma((n_row,)),
            dma((n_row,)),
            dma((2,)),
            dma((4,)),
            dma((4,)),
            dma((4,)),
            dma((4,)),
            dma((16,)),
            dma((16,)),
            dma((16,)),
            dma((16,)),
            dma((NG,)),
            dma((NG,)),
            dma((6,)),
            dma((n_row,)),
            dma((n_row,)),
            dma((n_col,)),
            dma((n_col,)),
            dma((n_row,)),
            dma((n_row,)),
        ],
        compiler_params=pltpu.CompilerParams(
            collective_id=0, has_side_effects=True, vmem_limit_bytes=60 * 1024 * 1024
        ),
    )(
        tokens,
        restype.reshape(1, 64),
        type_table,
        key_mask.reshape(1, 64),
        w_bias.T,
        cotangent,
        w_query,
        w_key,
        w_value,
        w_gate,
        pair,
    )
    return (token_grad, pair_grad, weight_grad.T)


def solution(mesh):
    placed = (
        P("samp", "col", None),
        P("col"),
        P(),
        P("col"),
        P("row", "col", None),
        P(),
        P(),
        P(),
        P(),
        P(),
        P("samp", "col", None),
    )
    return jax.shard_map(
        body,
        mesh=mesh,
        in_specs=placed,
        out_specs=(P("samp", "col", None), P("row", "col", None), P()),
        check_vma=False,
    )
```
